256 devices in a mesh: row: 16 (over z, y_lo), col: 16 (over x, y_hi, core).
Axes of the slice: x: 4, y: 4 (y_hi: 2, y_lo: 2; y = y_hi * 2 + y_lo), z: 8, core: 2. Of those that a mesh axis runs over, the one named last changes fastest.
Arguments:
- pair_rep: bfloat16 [768, 768, 128], P('row', 'col'), may hold values from -6 to 6
- tok_mask: int32 [768], replicated, may hold values 0 or 1
- windows: int32 [2, 2], replicated, may hold values from 0 to 15, as said below
- in_gain: float32 [2, 128], replicated, may hold values from 0.5 to 1.5
- in_bias: float32 [2, 128], replicated, may hold values from -3 to 3
- w_proj: bfloat16 [2, 128, 256], replicated, may hold values from -0.5 to 0.5
- w_gate: bfloat16 [2, 128, 256], replicated, may hold values from -0.5 to 0.5
- out_gain: float32 [2, 128], replicated, may hold values from 0.5 to 1.5
- out_bias: float32 [2, 128], replicated, may hold values from -3 to 3
- w_out: bfloat16 [2, 128, 128], replicated, may hold values from -0.5 to 0.5
- w_outgate: bfloat16 [2, 128, 128], replicated, may hold values from -0.5 to 0.5
Outputs:
- pair_out: bfloat16 [768, 768, 128], P('row', 'col')
The draws below stay inside these ranges and needn't reach their ends.
Inputs may be any that keep to these rules, and one draw needn't show every extreme that they name: windows[0,0] and windows[0,1] are two different column blocks below 16; windows[1,0] and windows[1,1] are two different row blocks below 16, one of them the last row block 15.
All inputs are finite; a program needn't handle non-finite values.
Results may differ from the reference program's by a relative error of at most 0.0055.
Values may be sent and summed in bfloat16 or wider, within the bound.
No kernel may reach another device: no remote copies, remote signals or barrier semaphores. Data moves between devices by JAX's collectives and lax.ppermute only.
A program may use at most 64 MiB of HBM per device.

```python
import jax
import jax.numpy as jnp
from jax import lax

C = 128
H = 128
TB = 48
TOKENS = 768
TI = 48
ROW_BLOCKS = 16
COL_BLOCKS = 16
N_ROW = 16


def draw_windows(key, part):
    key = jax.random.fold_in(key, 7)
    first_key, second_key, third_key = jax.random.split(key, 3)
    outgoing = jax.random.permutation(first_key, COL_BLOCKS)[:2]
    other_block = jax.random.randint(second_key, (), 0, ROW_BLOCKS - 1)
    last_block = jnp.array(ROW_BLOCKS - 1, dtype=jnp.int32)
    flip = jax.random.randint(third_key, (), 0, 2)
    first_in = jnp.where(flip == 0, other_block, last_block)
    second_in = jnp.where(flip == 0, last_block, other_block)
    incoming = jnp.stack([first_in, second_in])
    return jnp.stack([outgoing.astype(jnp.int32), incoming.astype(jnp.int32)]).astype(jnp.int32)


def set_ends(entries, rng, least, top_value):
    longest = entries.shape.index(max(entries.shape))
    spots = []
    for shift in (0, 1):
        where = [jax.random.randint(jax.random.fold_in(rng, axis), (), 0, length) for axis, length in enumerate(entries.shape)]
        where[longest] = (where[longest] + shift) % entries.shape[longest]
        spots.append(tuple(where))
    return entries.at[spots[0]].set(least).at[spots[1]].set(top_value)


def steps_of(rng, extent, cuts, least, largest):
    def one(axis_at, parts):
        heights = jax.random.uniform(jax.random.fold_in(jax.random.fold_in(rng, 6), axis_at), (parts,), jnp.float32, least / len(cuts), largest / len(cuts))
        return jnp.repeat(jnp.exp(heights), extent[axis_at] // parts).reshape((-1,) + (1,) * (len(extent) - axis_at - 1))

    factor_of = one(*cuts[0])
    for cut in cuts[1:]:
        factor_of = factor_of * one(*cut)
    return factor_of


def noise(stream_key, extent, deviation, limit, shards=(), kind=jnp.bfloat16):
    gain = steps_of(stream_key, extent, shards, -0.22, 0.18) if shards else 1.0
    result = jax.random.normal(stream_key, extent, jnp.float32) * deviation * gain
    return jnp.minimum(jnp.maximum(result, -limit), limit).astype(kind)


def setup_inputs(seed: int = 0) -> dict:
    arg_keys = jax.random.split(jax.random.key(seed), 12)
    pair_rep = noise(arg_keys[0], (TOKENS, TOKENS, C), 1.0, 6.0, ((0, 16), (1, 16)))
    tok_mask = set_ends((jax.random.randint(arg_keys[1], (TOKENS,), 0, 8) < 7).astype(jnp.int32), jax.random.fold_in(arg_keys[1], 1), 0, 1)
    windows = draw_windows(jax.random.fold_in(arg_keys[11], 71), 0)
    in_gain = jnp.clip(jax.random.uniform(arg_keys[3], (2, C), jnp.float32, 0.5, 1.5), 0.5, 1.5)
    in_bias = noise(arg_keys[4], (2, C), 0.5, 3.0, (), jnp.float32)
    w_proj = noise(arg_keys[5], (2, C, 2 * H), C ** -0.5, 0.5)
    w_gate = noise(arg_keys[6], (2, C, 2 * H), C ** -0.5, 0.5)
    out_gain = jnp.clip(jax.random.uniform(arg_keys[7], (2, H), jnp.float32, 0.5, 1.5), 0.5, 1.5)
    out_bias = noise(arg_keys[8], (2, H), 0.5, 3.0, (), jnp.float32)
    w_out = noise(arg_keys[9], (2, H, C), H ** -0.5, 0.5)
    w_outgate = noise(arg_keys[10], (2, C, C), C ** -0.5, 0.5)
    return dict(pair_rep=pair_rep, tok_mask=tok_mask, windows=windows, in_gain=in_gain, in_bias=in_bias, w_proj=w_proj, w_gate=w_gate, out_gain=out_gain, out_bias=out_bias, w_out=w_out, w_outgate=w_outgate)


def layer_norm(values, ln_gain, ln_bias):
    values = values.astype(jnp.float32)
    average = lax.optimization_barrier(jnp.mean(values, axis=-1, keepdims=True))
    centred = values - average
    variance = lax.optimization_barrier(jnp.mean(centred * centred, axis=-1, keepdims=True))
    return centred * lax.rsqrt(variance + 1e-05) * ln_gain + ln_bias

def gate_project(normed, row_keep, col_keep, weight_proj, weight_gate):
    flat = normed.reshape(-1, normed.shape[-1])
    projected = jnp.dot(flat, weight_proj, preferred_element_type=jnp.float32)
    gate_logit = jnp.dot(flat, weight_gate, preferred_element_type=jnp.float32)
    keep = (row_keep[:, None] * col_keep[None, :]).astype(jnp.float32).reshape(-1, 1)
    gated = jax.nn.sigmoid(gate_logit) * projected * keep
    return gated.astype(jnp.bfloat16).reshape(normed.shape[0], normed.shape[1], -1)

def finish(current, contracted, normed, out_gain, out_bias, w_out, w_outgate):
    shape = current.shape
    scaled = layer_norm(contracted, out_gain, out_bias).astype(jnp.bfloat16)
    branch = jnp.dot(scaled.reshape(-1, scaled.shape[-1]), w_out, preferred_element_type=jnp.float32)
    gate_logit = jnp.dot(normed.reshape(-1, normed.shape[-1]), w_outgate, preferred_element_type=jnp.float32)
    updated = current.reshape(-1, shape[-1]).astype(jnp.float32) + branch * jax.nn.sigmoid(gate_logit)
    return updated.astype(jnp.bfloat16).reshape(shape)

def reference(pair_rep, tok_mask, windows, in_gain, in_bias, w_proj, w_gate, out_gain, out_bias, w_out, w_outgate):
    current = pair_rep
    hidden = w_out.shape[1]
    starts = jnp.arange(N_ROW, dtype=jnp.int32) * TI
    for update in range(2):
        width = TB if update == 0 else TI
        axis_id = 1 - update
        pieces = []
        keeps = []
        for slot_idx in range(2):
            offset = (windows[update, slot_idx] * width).astype(jnp.int32)
            pieces.append(lax.dynamic_slice_in_dim(current, offset, width, axis_id))
            keeps.append(lax.dynamic_slice_in_dim(tok_mask, offset, width, 0))
        band = jnp.concatenate(pieces, axis=axis_id)
        band_keep = jnp.concatenate(keeps, axis=0)
        normed_band = layer_norm(band, in_gain[update], in_bias[update]).astype(jnp.bfloat16)
        if update == 0:
            gated = gate_project(normed_band, tok_mask, band_keep, w_proj[update], w_gate[update])
        else:
            gated = gate_project(normed_band, band_keep, tok_mask, w_proj[update], w_gate[update])
        left_side = gated[:, :, :hidden].astype(jnp.float32)
        right_side = gated[:, :, hidden:].astype(jnp.float32)
        state = current

        def row_block(start, update=update, state=state, left_side=left_side, right_side=right_side):
            rows = lax.dynamic_slice_in_dim(state, start, TI, 0)
            normed = layer_norm(rows, in_gain[update], in_bias[update]).astype(jnp.bfloat16)
            if update == 0:
                part = lax.dynamic_slice_in_dim(left_side, start, TI, 0)
                contracted = jnp.einsum('ikh,jkh->ijh', part, right_side, precision=lax.Precision.HIGHEST)
            else:
                part = lax.dynamic_slice_in_dim(left_side, start, TI, 1)
                contracted = jnp.einsum('kih,kjh->ijh', part, right_side, precision=lax.Precision.HIGHEST)
            return finish(rows, contracted, normed, out_gain[update], out_bias[update], w_out[update], w_outgate[update])
        blocks = lax.map(row_block, starts)
        current = blocks.reshape(current.shape)
    return current
```

```python
import jax
import jax.numpy as jnp
from jax import lax
from jax.sharding import PartitionSpec as P


def layer_norm(values, ln_gain, ln_bias):
    values = values.astype(jnp.float32)
    average = jnp.mean(values, axis=-1, keepdims=True)
    centred = values - average
    variance = jnp.mean(centred * centred, axis=-1, keepdims=True)
    return centred * lax.rsqrt(variance + 1e-05) * ln_gain + ln_bias


def gate_project(normed, keep, weight_proj, weight_gate):
    flat = normed.reshape(-1, normed.shape[-1])
    projected = jnp.dot(flat, weight_proj, preferred_element_type=jnp.float32)
    gate_logit = jnp.dot(flat, weight_gate, preferred_element_type=jnp.float32)
    gated = jax.nn.sigmoid(gate_logit) * projected * keep.astype(jnp.float32).reshape(-1, 1)
    return gated.astype(jnp.bfloat16).reshape(normed.shape[0], normed.shape[1], -1)


def finish(current, contracted, normed, out_gain, out_bias, w_out, w_outgate):
    shape = current.shape
    scaled = layer_norm(contracted, out_gain, out_bias).astype(jnp.bfloat16)
    branch = jnp.dot(
        scaled.reshape(-1, scaled.shape[-1]), w_out, preferred_element_type=jnp.float32
    )
    gate_logit = jnp.dot(
        normed.reshape(-1, normed.shape[-1]), w_outgate, preferred_element_type=jnp.float32
    )
    updated = current.reshape(-1, shape[-1]).astype(jnp.float32) + branch * jax.nn.sigmoid(
        gate_logit
    )
    return updated.astype(jnp.bfloat16).reshape(shape)


def gather(piece, axis):
    n = lax.axis_size(axis)
    copies = jnp.broadcast_to(piece[None], (n,) + piece.shape)
    return lax.all_to_all(copies, axis, 0, 0, tiled=True)


def body(
    pair_rep,
    tok_mask,
    windows,
    in_gain,
    in_bias,
    w_proj,
    w_gate,
    out_gain,
    out_bias,
    w_out,
    w_outgate,
):
    tile = pair_rep.shape[0]
    width = pair_rep.shape[2]
    hidden = w_out.shape[1]
    n = lax.axis_size("row")
    part = tile // n
    row_idx = lax.axis_index("row")
    col_idx = lax.axis_index("col")
    transposed = [(a * n + b, b * n + a) for a in range(n) for b in range(n)]
    current = pair_rep
    for update in range(2):
        normed = layer_norm(current, in_gain[update], in_bias[update]).astype(jnp.bfloat16)
        spread, here = ("col", row_idx) if update == 0 else ("row", col_idx)
        mine = lax.axis_index(spread)
        pieces = lax.all_to_all(current.reshape(n, part, tile, width), spread, 0, 0, tiled=True)
        band = [
            lax.dynamic_index_in_dim(pieces, windows[update, slot], 0, keepdims=False)
            for slot in range(2)
        ]
        keep = [
            lax.dynamic_slice_in_dim(tok_mask, windows[update, slot] * tile, tile)
            for slot in range(2)
        ]
        if update == 0:
            band = jnp.concatenate(band, axis=1)
            first_keep = lax.dynamic_slice_in_dim(tok_mask, here * tile + mine * part, part)
            second_keep = jnp.concatenate(keep)
        else:
            band = jnp.concatenate(band, axis=0)
            first_keep = jnp.concatenate(
                [lax.dynamic_slice_in_dim(k, mine * part, part) for k in keep]
            )
            second_keep = lax.dynamic_slice_in_dim(tok_mask, here * tile, tile)
        band_normed = layer_norm(band, in_gain[update], in_bias[update]).astype(jnp.bfloat16)
        both = first_keep[:, None] * second_keep[None, :]
        gated = gate_project(band_normed, both, w_proj[update], w_gate[update])
        left, right = gated[..., :hidden], gated[..., hidden:]
        if update == 0:
            right = lax.ppermute(right, ("row", "col"), transposed)
            left = gather(left, "col").reshape(tile, 2 * tile, hidden)
            right = gather(right, "row").reshape(tile, 2 * tile, hidden)
            contracted = jnp.einsum("ikh,jkh->ijh", left, right, preferred_element_type=jnp.float32)
        else:
            left = lax.ppermute(left, ("row", "col"), transposed)
            right = gather(right, "row").reshape(2 * tile, tile, hidden)
            left = gather(left, "col").reshape(2 * tile, tile, hidden)
            contracted = jnp.einsum("kih,kjh->ijh", left, right, preferred_element_type=jnp.float32)
        current = finish(
            current,
            contracted,
            normed,
            out_gain[update],
            out_bias[update],
            w_out[update],
            w_outgate[update],
        )
    return current


def solution(mesh):
    placed = (P("row", "col", None), P(), P(), P(), P(), P(), P(), P(), P(), P(), P())
    return jax.shard_map(
        body, mesh=mesh, in_specs=placed, out_specs=P("row", "col", None), check_vma=False
    )
```

```python
import jax
import jax.numpy as jnp
from jax import lax
from jax.sharding import PartitionSpec as P


def layer_norm(values, ln_gain, ln_bias):
    values = values.astype(jnp.float32)
    average = jnp.mean(values, axis=-1, keepdims=True)
    centred = values - average
    variance = jnp.mean(centred * centred, axis=-1, keepdims=True)
    return centred * lax.rsqrt(variance + 1e-05) * ln_gain + ln_bias


def gate_project(normed, keep, weight_proj, weight_gate):
    flat = normed.reshape(-1, normed.shape[-1])
    projected = jnp.dot(flat, weight_proj, preferred_element_type=jnp.float32)
    gate_logit = jnp.dot(flat, weight_gate, preferred_element_type=jnp.float32)
    gated = jax.nn.sigmoid(gate_logit) * projected * keep.astype(jnp.float32).reshape(-1, 1)
    return gated.astype(jnp.bfloat16).reshape(normed.shape[0], normed.shape[1], -1)


def finish(current, contracted, normed, out_gain, out_bias, w_out, w_outgate):
    shape = current.shape
    scaled = layer_norm(contracted, out_gain, out_bias).astype(jnp.bfloat16)
    branch = jnp.dot(
        scaled.reshape(-1, scaled.shape[-1]), w_out, preferred_element_type=jnp.float32
    )
    gate_logit = jnp.dot(
        normed.reshape(-1, normed.shape[-1]), w_outgate, preferred_element_type=jnp.float32
    )
    updated = current.reshape(-1, shape[-1]).astype(jnp.float32) + branch * jax.nn.sigmoid(
        gate_logit
    )
    return updated.astype(jnp.bfloat16).reshape(shape)


def swap(x, axis, bits):
    n = lax.axis_size(axis)
    return lax.ppermute(x, axis, [(p, p ^ bits) for p in range(n)])


def in_order(by_distance, place):
    count = len(by_distance)
    rows = []
    for p in range(count):
        row = by_distance[p]
        for q in range(1, count):
            row = jnp.where(place == q, by_distance[p ^ q], row)
        rows.append(row)
    return jnp.stack(rows)


def gather_col(piece):
    col = lax.axis_index("col")
    x, half, core = col // 4, (col // 2) % 2, col % 2
    pair = in_order([piece, swap(piece, "col", 2)], half)
    four = in_order([pair] + [swap(pair, "col", 4 * d) for d in (1, 2, 3)], x)
    both = in_order([four, swap(four, "col", 1)], core)
    return jnp.moveaxis(both, 0, 2).reshape((16,) + piece.shape)


def transpose_devices(x):
    n = lax.axis_size("row")
    pairs = [(a * n + b, b * n + a) for a in range(n) for b in range(n)]
    return lax.ppermute(x, ("row", "col"), pairs)


def body(
    pair_rep,
    tok_mask,
    windows,
    in_gain,
    in_bias,
    w_proj,
    w_gate,
    out_gain,
    out_bias,
    w_out,
    w_outgate,
):
    tile = pair_rep.shape[0]
    width = pair_rep.shape[2]
    hidden = w_out.shape[1]
    n = lax.axis_size("row")
    part = tile // n
    row_idx = lax.axis_index("row")
    col_idx = lax.axis_index("col")

    def pick(stacked, update):
        return [
            lax.dynamic_index_in_dim(stacked, windows[update, slot], 0, keepdims=False)
            for slot in range(2)
        ]

    def norm_in(values, update):
        return layer_norm(values, in_gain[update], in_bias[update]).astype(jnp.bfloat16)

    def end(current, contracted, normed, update):
        return finish(
            current,
            contracted,
            normed,
            out_gain[update],
            out_bias[update],
            w_out[update],
            w_outgate[update],
        )

    keeps = tok_mask.reshape(n, tile)
    row_keep = lax.dynamic_index_in_dim(keeps, row_idx, 0, keepdims=False)
    col_keep = lax.dynamic_index_in_dim(keeps, col_idx, 0, keepdims=False)
    window_keep = [jnp.concatenate(pick(keeps, update)) for update in range(2)]

    pieces = lax.all_to_all(pair_rep.reshape(n, part, tile, width), "col", 0, 0, tiled=True)
    band = jnp.concatenate(pick(pieces, 0), axis=1)
    part_keep = lax.dynamic_slice_in_dim(row_keep, col_idx * part, part)
    gated = gate_project(
        norm_in(band, 0), part_keep[:, None] * window_keep[0][None, :], w_proj[0], w_gate[0]
    )
    left_own, right_own = gated[..., :hidden], gated[..., hidden:]
    moved = transpose_devices(jnp.stack([left_own, right_own]))

    rows = pair_rep.reshape(n, part, tile, width)
    chunks = jnp.concatenate([jnp.broadcast_to(moved[1], (n,) + moved[1].shape), rows], axis=2)
    chunks = lax.all_to_all(chunks, "row", 0, 0, tiled=True)
    right = chunks[:, :, : 2 * tile].reshape(tile, 2 * tile, hidden)
    rows = jnp.concatenate(pick(chunks[:, :, 2 * tile :], 1), axis=0)
    lefts = gather_col(jnp.stack([left_own, moved[0]]))
    left = lefts[:, 0].reshape(tile, 2 * tile, hidden)
    left_rows = jnp.concatenate(pick(lefts[:, 1], 1), axis=0)

    contracted = jnp.einsum("ikh,jkh->ijh", left_rows, right, preferred_element_type=jnp.float32)
    rows = end(rows, contracted, norm_in(rows, 0), 0)
    rows_keep = jnp.concatenate(
        [lax.dynamic_slice_in_dim(k, row_idx * part, part) for k in pick(keeps, 1)]
    )
    gated = gate_project(
        norm_in(rows, 1), rows_keep[:, None] * col_keep[None, :], w_proj[1], w_gate[1]
    )
    next_left = transpose_devices(gated[..., :hidden])
    next_left, left = lax.optimization_barrier((next_left, left))
    copies = jnp.broadcast_to(gated[..., hidden:], (n, 2 * part, tile, hidden))
    next_right = lax.all_to_all(copies, "row", 0, 0, tiled=True).reshape(2 * tile, tile, hidden)

    contracted = jnp.einsum("ikh,jkh->ijh", left, right, preferred_element_type=jnp.float32)
    current = end(pair_rep, contracted, norm_in(pair_rep, 0), 0)

    next_left = gather_col(next_left).reshape(2 * tile, tile, hidden)
    contracted = jnp.einsum(
        "kih,kjh->ijh", next_left, next_right, preferred_element_type=jnp.float32
    )
    return end(current, contracted, norm_in(current, 1), 1)


def solution(mesh):
    placed = (P("row", "col", None), P(), P(), P(), P(), P(), P(), P(), P(), P(), P())
    return jax.shard_map(
        body, mesh=mesh, in_specs=placed, out_specs=P("row", "col", None), check_vma=False
    )
```

```python
import jax
import jax.numpy as jnp
from jax import lax
from jax.sharding import PartitionSpec as P


def layer_norm(values, ln_gain, ln_bias):
    values = values.astype(jnp.float32)
    average = jnp.mean(values, axis=-1, keepdims=True)
    centred = values - average
    variance = jnp.mean(centred * centred, axis=-1, keepdims=True)
    return centred * lax.rsqrt(variance + 1e-05) * ln_gain + ln_bias


def gate_project(normed, keep, weight_proj, weight_gate):
    flat = normed.reshape(-1, normed.shape[-1])
    projected = jnp.dot(flat, weight_proj, preferred_element_type=jnp.float32)
    gate_logit = jnp.dot(flat, weight_gate, preferred_element_type=jnp.float32)
    gated = jax.nn.sigmoid(gate_logit) * projected * keep.astype(jnp.float32).reshape(-1, 1)
    return gated.astype(jnp.bfloat16).reshape(normed.shape[0], normed.shape[1], -1)


def out_gate(normed, w_outgate):
    flat = normed.reshape(-1, normed.shape[-1])
    return jax.nn.sigmoid(jnp.dot(flat, w_outgate, preferred_element_type=jnp.float32))


def finish(current, contracted, gate, out_gain, out_bias, w_out):
    shape = current.shape
    scaled = layer_norm(contracted, out_gain, out_bias).astype(jnp.bfloat16)
    branch = jnp.dot(
        scaled.reshape(-1, scaled.shape[-1]), w_out, preferred_element_type=jnp.float32
    )
    updated = current.reshape(-1, shape[-1]).astype(jnp.float32) + branch * gate
    return updated.astype(jnp.bfloat16).reshape(shape)


def swap(x, axis, bits):
    n = lax.axis_size(axis)
    return lax.ppermute(x, axis, [(p, p ^ bits) for p in range(n)])


def put(buffer, x, *at):
    return lax.dynamic_update_slice(buffer, x.reshape((1,) * len(at) + x.shape), at + (0,) * x.ndim)


def gather_col(piece, meanwhile):
    col = lax.axis_index("col")
    x, half, core = col // 4, (col // 2) % 2, col % 2
    pair = jnp.zeros((2,) + piece.shape, piece.dtype)
    pair = put(put(pair, piece, half), swap(piece, "col", 2), 1 - half)
    pair, meanwhile = lax.optimization_barrier((pair, meanwhile))
    four = put(jnp.zeros((4,) + pair.shape, piece.dtype), pair, x)
    for d in (2, 1, 3):
        four = put(four, swap(pair, "col", 4 * d), x ^ d)
    whole = jnp.zeros((2,) + four.shape, piece.dtype)
    whole = put(put(whole, four, core), swap(four, "col", 1), 1 - core)
    return jnp.moveaxis(whole, 0, 2).reshape((16,) + piece.shape), meanwhile


def transpose_devices(x):
    n = lax.axis_size("row")
    pairs = [(a * n + b, b * n + a) for a in range(n) for b in range(n)]
    return lax.ppermute(x, ("row", "col"), pairs)


def body(
    pair_rep,
    tok_mask,
    windows,
    in_gain,
    in_bias,
    w_proj,
    w_gate,
    out_gain,
    out_bias,
    w_out,
    w_outgate,
):
    tile = pair_rep.shape[0]
    width = pair_rep.shape[2]
    hidden = w_out.shape[1]
    n = lax.axis_size("row")
    part = tile // n
    row_idx = lax.axis_index("row")
    col_idx = lax.axis_index("col")

    def pick(stacked, update):
        return [
            lax.dynamic_index_in_dim(stacked, windows[update, slot], 0, keepdims=False)
            for slot in range(2)
        ]

    def norm_in(values, update):
        return layer_norm(values, in_gain[update], in_bias[update]).astype(jnp.bfloat16)

    def gate_of(normed, update):
        return out_gate(normed, w_outgate[update])

    def end(current, contracted, gate, update):
        return finish(current, contracted, gate, out_gain[update], out_bias[update], w_out[update])

    keeps = tok_mask.reshape(n, tile)
    row_keep = lax.dynamic_index_in_dim(keeps, row_idx, 0, keepdims=False)
    col_keep = lax.dynamic_index_in_dim(keeps, col_idx, 0, keepdims=False)
    window_keep = [jnp.concatenate(pick(keeps, update)) for update in range(2)]

    pieces = lax.all_to_all(pair_rep.reshape(n, part, tile, width), "col", 0, 0, tiled=True)
    gate = gate_of(norm_in(pair_rep, 0), 0)
    pieces, gate = lax.optimization_barrier((pieces, gate))
    band = jnp.concatenate(pick(pieces, 0), axis=1)
    part_keep = lax.dynamic_slice_in_dim(row_keep, col_idx * part, part)
    gated = gate_project(
        norm_in(band, 0), part_keep[:, None] * window_keep[0][None, :], w_proj[0], w_gate[0]
    )
    left_own, right_own = gated[..., :hidden], gated[..., hidden:]
    moved = transpose_devices(jnp.stack([left_own, right_own]))

    rows = pair_rep.reshape(n, part, tile, width)
    chunks = jnp.concatenate([jnp.broadcast_to(moved[1], (n,) + moved[1].shape), rows], axis=2)
    lefts = jnp.stack([left_own, moved[0]])
    chunks, lefts = lax.optimization_barrier((chunks, lefts))
    chunks = lax.all_to_all(chunks, "row", 0, 0, tiled=True)
    right = chunks[:, :, : 2 * tile].reshape(tile, 2 * tile, hidden)
    rows = jnp.concatenate(pick(chunks[:, :, 2 * tile :], 1), axis=0)
    lefts, _ = gather_col(lefts, ())
    left = lefts[:, 0].reshape(tile, 2 * tile, hidden)
    left_rows = jnp.concatenate(pick(lefts[:, 1], 1), axis=0)

    contracted = jnp.einsum("ikh,jkh->ijh", left_rows, right, preferred_element_type=jnp.float32)
    rows = end(rows, contracted, gate_of(norm_in(rows, 0), 0), 0)
    rows_keep = jnp.concatenate(
        [lax.dynamic_slice_in_dim(k, row_idx * part, part) for k in pick(keeps, 1)]
    )
    gated = gate_project(
        norm_in(rows, 1), rows_keep[:, None] * col_keep[None, :], w_proj[1], w_gate[1]
    )
    next_left = transpose_devices(gated[..., :hidden])
    copies = jnp.broadcast_to(gated[..., hidden:], (n, 2 * part, tile, hidden))
    next_right = lax.all_to_all(copies, "row", 0, 0, tiled=True).reshape(2 * tile, tile, hidden)
    next_left, left = gather_col(next_left, left)
    next_left = next_left.reshape(2 * tile, tile, hidden)

    contracted = jnp.einsum("ikh,jkh->ijh", left, right, preferred_element_type=jnp.float32)
    current = end(pair_rep, contracted, gate, 0)

    contracted = jnp.einsum(
        "kih,kjh->ijh", next_left, next_right, preferred_element_type=jnp.float32
    )
    return end(current, contracted, gate_of(norm_in(current, 1), 1), 1)


def solution(mesh):
    placed = (P("row", "col", None), P(), P(), P(), P(), P(), P(), P(), P(), P(), P())
    return jax.shard_map(
        body, mesh=mesh, in_specs=placed, out_specs=P("row", "col", None), check_vma=False
    )
```

```python
import jax
import jax.numpy as jnp
from jax import lax
from jax.sharding import PartitionSpec as P


def layer_norm(values, ln_gain, ln_bias):
    values = values.astype(jnp.float32)
    average = jnp.mean(values, axis=-1, keepdims=True)
    centred = values - average
    variance = jnp.mean(centred * centred, axis=-1, keepdims=True)
    return centred * lax.rsqrt(variance + 1e-05) * ln_gain + ln_bias


def gate_project(normed, keep, weight_proj, weight_gate):
    flat = normed.reshape(-1, normed.shape[-1])
    projected = jnp.dot(flat, weight_proj, preferred_element_type=jnp.float32)
    gate_logit = jnp.dot(flat, weight_gate, preferred_element_type=jnp.float32)
    gated = jax.nn.sigmoid(gate_logit) * projected * keep.astype(jnp.float32).reshape(-1, 1)
    return gated.astype(jnp.bfloat16).reshape(normed.shape[0], normed.shape[1], -1)


def out_gate(normed, w_outgate):
    flat = normed.reshape(-1, normed.shape[-1])
    return jax.nn.sigmoid(jnp.dot(flat, w_outgate, preferred_element_type=jnp.float32))


def finish(current, contracted, gate, out_gain, out_bias, w_out):
    average = jnp.mean(contracted, axis=0, keepdims=True)
    centred = contracted - average
    variance = jnp.mean(centred * centred, axis=0, keepdims=True)
    scaled = centred * lax.rsqrt(variance + 1e-05) * out_gain[:, None, None] + out_bias[:, None, None]
    branch = jnp.einsum(
        "hij,hc->ijc", scaled.astype(jnp.bfloat16), w_out, preferred_element_type=jnp.float32
    )
    updated = current.astype(jnp.float32) + branch * gate.reshape(branch.shape)
    return updated.astype(jnp.bfloat16)


def swap(x, axis, bits):
    n = lax.axis_size(axis)
    return lax.ppermute(x, axis, [(p, p ^ bits) for p in range(n)])


def put(buffer, x, *at):
    return lax.dynamic_update_slice(buffer, x.reshape((1,) * len(at) + x.shape), at + (0,) * x.ndim)


def gather_col(piece, meanwhile):
    col = lax.axis_index("col")
    x, half, core = col // 4, (col // 2) % 2, col % 2
    pair = jnp.zeros((2,) + piece.shape, piece.dtype)
    pair = put(put(pair, piece, half), swap(piece, "col", 2), 1 - half)
    pair, meanwhile = lax.optimization_barrier((pair, meanwhile))
    four = put(jnp.zeros((4,) + pair.shape, piece.dtype), pair, x)
    for d in (2, 1, 3):
        four = put(four, swap(pair, "col", 4 * d), x ^ d)
    whole = jnp.zeros((2,) + four.shape, piece.dtype)
    whole = put(put(whole, four, core), swap(four, "col", 1), 1 - core)
    return jnp.moveaxis(whole, 0, 2).reshape((16,) + piece.shape), meanwhile


def transpose_devices(x):
    n = lax.axis_size("row")
    pairs = [(a * n + b, b * n + a) for a in range(n) for b in range(n)]
    return lax.ppermute(x, ("row", "col"), pairs)


def body(
    pair_rep,
    tok_mask,
    windows,
    in_gain,
    in_bias,
    w_proj,
    w_gate,
    out_gain,
    out_bias,
    w_out,
    w_outgate,
):
    tile = pair_rep.shape[0]
    width = pair_rep.shape[2]
    hidden = w_out.shape[1]
    n = lax.axis_size("row")
    part = tile // n
    row_idx = lax.axis_index("row")
    col_idx = lax.axis_index("col")

    def pick(stacked, update):
        return [
            lax.dynamic_index_in_dim(stacked, windows[update, slot], 0, keepdims=False)
            for slot in range(2)
        ]

    def norm_in(values, update):
        return layer_norm(values, in_gain[update], in_bias[update]).astype(jnp.bfloat16)

    def gate_of(normed, update):
        return out_gate(normed, w_outgate[update])

    def end(current, contracted, gate, update):
        return finish(current, contracted, gate, out_gain[update], out_bias[update], w_out[update])

    keeps = tok_mask.reshape(n, tile)
    row_keep = lax.dynamic_index_in_dim(keeps, row_idx, 0, keepdims=False)
    col_keep = lax.dynamic_index_in_dim(keeps, col_idx, 0, keepdims=False)
    window_keep = [jnp.concatenate(pick(keeps, update)) for update in range(2)]

    pieces = lax.all_to_all(pair_rep.reshape(n, part, tile, width), "col", 0, 0, tiled=True)
    band = jnp.concatenate(pick(pieces, 0), axis=1)
    part_keep = lax.dynamic_slice_in_dim(row_keep, col_idx * part, part)
    gated = gate_project(
        norm_in(band, 0), part_keep[:, None] * window_keep[0][None, :], w_proj[0], w_gate[0]
    )
    left_own, right_own = gated[..., :hidden], gated[..., hidden:]
    right_moved = transpose_devices(right_own)
    left_moved = transpose_devices(left_own)
    source, _ = lax.optimization_barrier((pair_rep, gated))
    gate = gate_of(norm_in(source, 0), 0)
    right_moved, gate = lax.optimization_barrier((right_moved, gate))

    rows = pair_rep.reshape(n, part, tile, width)
    chunks = jnp.concatenate([jnp.broadcast_to(right_moved, (n,) + right_moved.shape), rows], axis=2)
    chunks, left_own = lax.optimization_barrier((chunks, left_own))
    chunks = lax.all_to_all(chunks, "row", 0, 0, tiled=True)
    right = chunks[:, :, : 2 * tile].reshape(tile, 2 * tile, hidden)
    rows = jnp.concatenate(pick(chunks[:, :, 2 * tile :], 1), axis=0)
    lefts, _ = gather_col(jnp.stack([left_own, left_moved]), ())
    left = lefts[:, 0].reshape(tile, 2 * tile, hidden)
    left_rows = jnp.concatenate(pick(lefts[:, 1], 1), axis=0)

    contracted = jnp.einsum("ikh,jkh->hij", left_rows, right, preferred_element_type=jnp.float32)
    rows = end(rows, contracted, gate_of(norm_in(rows, 0), 0), 0)
    rows_keep = jnp.concatenate(
        [lax.dynamic_slice_in_dim(k, row_idx * part, part) for k in pick(keeps, 1)]
    )
    gated = gate_project(
        norm_in(rows, 1), rows_keep[:, None] * col_keep[None, :], w_proj[1], w_gate[1]
    )
    next_left = transpose_devices(gated[..., :hidden])
    copies = jnp.broadcast_to(gated[..., hidden:], (n, 2 * part, tile, hidden))
    next_right = lax.all_to_all(copies, "row", 0, 0, tiled=True).reshape(2 * tile, tile, hidden)
    next_left, left = gather_col(next_left, left)
    next_left = next_left.reshape(2 * tile, tile, hidden)

    contracted = jnp.einsum("ikh,jkh->hij", left, right, preferred_element_type=jnp.float32)
    current = end(pair_rep, contracted, gate, 0)

    contracted = jnp.einsum(
        "kih,kjh->hij", next_left, next_right, preferred_element_type=jnp.float32
    )
    return end(current, contracted, gate_of(norm_in(current, 1), 1), 1)


def solution(mesh):
    placed = (P("row", "col", None), P(), P(), P(), P(), P(), P(), P(), P(), P(), P())
    return jax.shard_map(
        body, mesh=mesh, in_specs=placed, out_specs=P("row", "col", None), check_vma=False
    )
```

```python
import jax
import jax.numpy as jnp
from jax import lax
from jax.sharding import PartitionSpec as P


def layer_norm(values, ln_gain, ln_bias):
    values = values.astype(jnp.float32)
    average = jnp.mean(values, axis=-1, keepdims=True)
    centred = values - average
    variance = jnp.mean(centred * centred, axis=-1, keepdims=True)
    return centred * lax.rsqrt(variance + 1e-05) * ln_gain + ln_bias


def gate_project(normed, keep, weight_proj, weight_gate):
    flat = normed.reshape(-1, normed.shape[-1])
    projected = jnp.dot(flat, weight_proj, preferred_element_type=jnp.float32)
    gate_logit = jnp.dot(flat, weight_gate, preferred_element_type=jnp.float32)
    gated = jax.nn.sigmoid(gate_logit) * projected * keep.astype(jnp.float32).reshape(-1, 1)
    return gated.astype(jnp.bfloat16).reshape(normed.shape[0], normed.shape[1], -1)


def out_gate(normed, w_outgate):
    flat = normed.reshape(-1, normed.shape[-1])
    return jax.nn.sigmoid(jnp.dot(flat, w_outgate, preferred_element_type=jnp.float32))


def finish(current, contracted, gate, out_gain, out_bias, w_out):
    average = jnp.mean(contracted, axis=0, keepdims=True)
    centred = contracted - average
    variance = jnp.mean(centred * centred, axis=0, keepdims=True)
    scaled = centred * lax.rsqrt(variance + 1e-05) * out_gain[:, None, None] + out_bias[:, None, None]
    branch = jnp.einsum(
        "hij,hc->ijc", scaled.astype(jnp.bfloat16), w_out, preferred_element_type=jnp.float32
    )
    updated = current.astype(jnp.float32) + branch * gate.reshape(branch.shape)
    return updated.astype(jnp.bfloat16)


def swap(x, axis, bits):
    n = lax.axis_size(axis)
    return lax.ppermute(x, axis, [(p, p ^ bits) for p in range(n)])


def put(buffer, x, *at):
    return lax.dynamic_update_slice(buffer, x.reshape((1,) * len(at) + x.shape), at + (0,) * x.ndim)


def gather_col(piece, meanwhile=(), second=lambda x: x):
    col = lax.axis_index("col")
    x, half, core = col // 4, (col // 2) % 2, col % 2
    pair = jnp.zeros((2,) + piece.shape, piece.dtype)
    pair = put(put(pair, piece, half), swap(piece, "col", 2), 1 - half)
    pair, meanwhile = lax.optimization_barrier((pair, meanwhile))
    four = put(jnp.zeros((4,) + pair.shape, piece.dtype), pair, x)
    for d in (2, 1, 3):
        four = put(four, swap(pair, "col", 4 * d), x ^ d)
    four, meanwhile = lax.optimization_barrier((four, second(meanwhile)))
    whole = jnp.zeros((2,) + four.shape, piece.dtype)
    whole = put(put(whole, four, core), swap(four, "col", 1), 1 - core)
    return jnp.moveaxis(whole, 0, 2).reshape((16,) + piece.shape), meanwhile


def transpose_devices(x):
    n = lax.axis_size("row")
    pairs = [(a * n + b, b * n + a) for a in range(n) for b in range(n)]
    return lax.ppermute(x, ("row", "col"), pairs)


def body(
    pair_rep,
    tok_mask,
    windows,
    in_gain,
    in_bias,
    w_proj,
    w_gate,
    out_gain,
    out_bias,
    w_out,
    w_outgate,
):
    tile = pair_rep.shape[0]
    width = pair_rep.shape[2]
    hidden = w_out.shape[1]
    n = lax.axis_size("row")
    part = tile // n
    row_idx = lax.axis_index("row")
    col_idx = lax.axis_index("col")

    def pick(stacked, update):
        return [
            lax.dynamic_index_in_dim(stacked, windows[update, slot], 0, keepdims=False)
            for slot in range(2)
        ]

    def norm_in(values, update):
        return layer_norm(values, in_gain[update], in_bias[update]).astype(jnp.bfloat16)

    def gate_of(normed, update):
        return out_gate(normed, w_outgate[update])

    def end(current, contracted, gate, update):
        return finish(current, contracted, gate, out_gain[update], out_bias[update], w_out[update])

    keeps = tok_mask.reshape(n, tile)
    row_keep = lax.dynamic_index_in_dim(keeps, row_idx, 0, keepdims=False)
    col_keep = lax.dynamic_index_in_dim(keeps, col_idx, 0, keepdims=False)
    window_keep = [jnp.concatenate(pick(keeps, update)) for update in range(2)]

    pieces = lax.all_to_all(pair_rep.reshape(n, part, tile, width), "col", 0, 0, tiled=True)
    band = jnp.concatenate(pick(pieces, 0), axis=1)
    part_keep = lax.dynamic_slice_in_dim(row_keep, col_idx * part, part)
    gated = gate_project(
        norm_in(band, 0), part_keep[:, None] * window_keep[0][None, :], w_proj[0], w_gate[0]
    )
    left_own, right_own = gated[..., :hidden], gated[..., hidden:]
    right_moved = transpose_devices(right_own)
    left_moved = transpose_devices(left_own)
    source, _ = lax.optimization_barrier((pair_rep, gated))
    gate = gate_of(norm_in(source, 0), 0)
    right_moved, gate = lax.optimization_barrier((right_moved, gate))

    rows = pair_rep.reshape(n, part, tile, width)
    chunks = jnp.concatenate([jnp.broadcast_to(right_moved, (n,) + right_moved.shape), rows], axis=2)
    chunks, left_own = lax.optimization_barrier((chunks, left_own))
    chunks = lax.all_to_all(chunks, "row", 0, 0, tiled=True)
    right = chunks[:, :, : 2 * tile].reshape(tile, 2 * tile, hidden)
    rows = jnp.concatenate(pick(chunks[:, :, 2 * tile :], 1), axis=0)
    lefts, _ = gather_col(jnp.stack([left_own, left_moved]))
    left = lefts[:, 0].reshape(tile, 2 * tile, hidden)
    left_rows = jnp.concatenate(pick(lefts[:, 1], 1), axis=0)

    contracted = jnp.einsum("ikh,jkh->hij", left_rows, right, preferred_element_type=jnp.float32)
    rows = end(rows, contracted, gate_of(norm_in(rows, 0), 0), 0)
    rows_keep = jnp.concatenate(
        [lax.dynamic_slice_in_dim(k, row_idx * part, part) for k in pick(keeps, 1)]
    )
    gated = gate_project(
        norm_in(rows, 1), rows_keep[:, None] * col_keep[None, :], w_proj[1], w_gate[1]
    )
    next_left = transpose_devices(gated[..., :hidden])
    copies = jnp.broadcast_to(gated[..., hidden:], (n, 2 * part, tile, hidden))
    next_right = lax.all_to_all(copies, "row", 0, 0, tiled=True).reshape(2 * tile, tile, hidden)
    next_left, contracted = gather_col(
        next_left,
        left,
        lambda x: jnp.einsum("ikh,jkh->hij", x, right, preferred_element_type=jnp.float32),
    )
    next_left = next_left.reshape(2 * tile, tile, hidden)
    current = end(pair_rep, contracted, gate, 0)

    contracted = jnp.einsum(
        "kih,kjh->hij", next_left, next_right, preferred_element_type=jnp.float32
    )
    return end(current, contracted, gate_of(norm_in(current, 1), 1), 1)


def solution(mesh):
    placed = (P("row", "col", None), P(), P(), P(), P(), P(), P(), P(), P(), P(), P())
    return jax.shard_map(
        body, mesh=mesh, in_specs=placed, out_specs=P("row", "col", None), check_vma=False
    )
```

```python
import jax
import jax.numpy as jnp
from jax import lax
from jax.sharding import PartitionSpec as P


def layer_norm(values, ln_gain, ln_bias):
    values = values.astype(jnp.float32)
    average = jnp.mean(values, axis=-1, keepdims=True)
    centred = values - average
    variance = jnp.mean(centred * centred, axis=-1, keepdims=True)
    return centred * lax.rsqrt(variance + 1e-05) * ln_gain + ln_bias


def gate_project(normed, keep, weight_proj, weight_gate):
    flat = normed.reshape(-1, normed.shape[-1])
    projected = jnp.dot(flat, weight_proj, preferred_element_type=jnp.float32)
    gate_logit = jnp.dot(flat, weight_gate, preferred_element_type=jnp.float32)
    gated = jax.nn.sigmoid(gate_logit) * projected * keep
    return gated.astype(jnp.bfloat16).reshape(normed.shape[0], normed.shape[1], -1)


def out_gate(normed, w_outgate):
    flat = normed.reshape(-1, normed.shape[-1])
    return jax.nn.sigmoid(jnp.dot(flat, w_outgate, preferred_element_type=jnp.float32))


def rescale(contracted, out_gain, out_bias):
    average = jnp.mean(contracted, axis=0, keepdims=True)
    centred = contracted - average
    variance = jnp.mean(centred * centred, axis=0, keepdims=True)
    scaled = centred * lax.rsqrt(variance + 1e-05) * out_gain[:, None, None] + out_bias[:, None, None]
    return scaled.astype(jnp.bfloat16)


def finish(current, scaled, gate, w_out):
    branch = jnp.einsum("hij,hc->ijc", scaled, w_out, preferred_element_type=jnp.float32)
    updated = current.astype(jnp.float32) + branch * gate.reshape(branch.shape)
    return updated.astype(jnp.bfloat16)


def swap(x, axis, bits):
    n = lax.axis_size(axis)
    return lax.ppermute(x, axis, [(p, p ^ bits) for p in range(n)])


def put(buffer, x, *at):
    at = at + (jnp.uint32(0),) * x.ndim
    return lax.dynamic_update_slice(buffer, x.reshape((1,) * (len(at) - x.ndim) + x.shape), at)


def gather_col(piece, places, meanwhile=(), second=lambda x: x):
    half, other_half, ring, core, other_core = places
    pair = jnp.zeros((2,) + piece.shape, piece.dtype)
    pair = put(put(pair, piece, half), swap(piece, "col", 2), other_half)
    pair, meanwhile = lax.optimization_barrier((pair, meanwhile))
    four = put(jnp.zeros((4,) + pair.shape, piece.dtype), pair, ring[0])
    for d in (2, 1, 3):
        four = put(four, swap(pair, "col", 4 * d), ring[d])
    four, meanwhile = lax.optimization_barrier((four, second(meanwhile)))
    whole = jnp.zeros((2,) + four.shape, piece.dtype)
    whole = put(put(whole, four, core), swap(four, "col", 1), other_core)
    return jnp.moveaxis(whole, 0, 2).reshape((16,) + piece.shape), meanwhile


def transpose_devices(x):
    n = lax.axis_size("row")
    pairs = [(a * n + b, b * n + a) for a in range(n) for b in range(n)]
    return lax.ppermute(x, ("row", "col"), pairs)


def body(
    pair_rep,
    tok_mask,
    windows,
    in_gain,
    in_bias,
    w_proj,
    w_gate,
    out_gain,
    out_bias,
    w_out,
    w_outgate,
):
    tile = pair_rep.shape[0]
    width = pair_rep.shape[2]
    hidden = w_out.shape[1]
    n = lax.axis_size("row")
    part = tile // n
    row = lax.axis_index("row").astype(jnp.uint32)
    col = lax.axis_index("col").astype(jnp.uint32)
    wanted = windows.astype(jnp.uint32)
    zero = jnp.uint32(0)

    def pick(stacked, update):
        sizes = (1,) + stacked.shape[1:]
        return [
            lax.dynamic_slice(
                stacked, (wanted[update, slot],) + (zero,) * (stacked.ndim - 1), sizes
            )[0]
            for slot in range(2)
        ]

    def norm_in(values, update):
        return layer_norm(values, in_gain[update], in_bias[update]).astype(jnp.bfloat16)

    def gate_of(normed, update):
        return out_gate(normed, w_outgate[update])

    def scale(contracted, update):
        return rescale(contracted, out_gain[update], out_bias[update])

    keeps = tok_mask.astype(jnp.float32).reshape(n, tile)
    row_keep = lax.dynamic_slice(keeps, (row, zero), (1, tile))[0]
    col_keep = lax.dynamic_slice(keeps, (col, zero), (1, tile))[0]
    part_keep = lax.dynamic_slice(row_keep, (col * part,), (part,))
    band_keep = part_keep[:, None] * jnp.concatenate(pick(keeps, 0))[None, :]
    rows_keep = [lax.dynamic_slice(k, (row * part,), (part,)) for k in pick(keeps, 1)]
    rows_keep = jnp.concatenate(rows_keep)[:, None] * col_keep[None, :]
    half, core = (col >> 1) & 1, col & 1
    places = (half, half ^ 1, [(col >> 2) ^ d for d in range(4)], core, core ^ 1)

    pieces = lax.all_to_all(pair_rep.reshape(n, part, tile, width), "col", 0, 0, tiled=True)
    pieces, places, band_keep, rows_keep = lax.optimization_barrier(
        (pieces, places, band_keep.reshape(-1, 1), rows_keep.reshape(-1, 1))
    )
    band = jnp.concatenate(pick(pieces, 0), axis=1)
    gated = gate_project(norm_in(band, 0), band_keep, w_proj[0], w_gate[0])
    left_own, right_own = gated[..., :hidden], gated[..., hidden:]
    right_moved = transpose_devices(right_own)
    left_moved = transpose_devices(left_own)
    source, _ = lax.optimization_barrier((pair_rep, gated))
    gate = gate_of(norm_in(source, 0), 0)
    right_moved, gate = lax.optimization_barrier((right_moved, gate))
    rows = pair_rep.reshape(n, part, tile, width)
    chunks = jnp.concatenate([jnp.broadcast_to(right_moved, (n,) + right_moved.shape), rows], axis=2)
    chunks, left_own = lax.optimization_barrier((chunks, left_own))
    chunks = lax.all_to_all(chunks, "row", 0, 0, tiled=True)
    lefts, _ = gather_col(jnp.stack([left_own, left_moved]), places)
    left = lefts[:, 0].reshape(tile, 2 * tile, hidden)
    left_rows = jnp.concatenate(pick(lefts[:, 1], 1), axis=0)
    right = chunks[:, :, : 2 * tile].reshape(tile, 2 * tile, hidden)
    rows = jnp.concatenate(pick(chunks[:, :, 2 * tile :], 1), axis=0)

    def contract(x):
        return jnp.einsum("ikh,jkh->hij", x, right, preferred_element_type=jnp.float32)

    scaled = scale(contract(left_rows), 0)
    rows = finish(rows, scaled, gate_of(norm_in(rows, 0), 0), w_out[0])
    gated = gate_project(norm_in(rows, 1), rows_keep, w_proj[1], w_gate[1])
    next_left = transpose_devices(gated[..., :hidden])
    copies = jnp.broadcast_to(gated[..., hidden:], (n, 2 * part, tile, hidden))
    next_right = lax.all_to_all(copies, "row", 0, 0, tiled=True).reshape(2 * tile, tile, hidden)

    next_left, scaled = gather_col(next_left, places, left, lambda x: scale(contract(x), 0))
    current = finish(pair_rep, scaled, gate, w_out[0])
    gate = gate_of(norm_in(current, 1), 1)

    next_left = next_left.reshape(2 * tile, tile, hidden)
    contracted = jnp.einsum(
        "kih,kjh->hij", next_left, next_right, preferred_element_type=jnp.float32
    )
    return finish(current, scale(contracted, 1), gate, w_out[1])


def solution(mesh):
    placed = (P("row", "col", None), P(), P(), P(), P(), P(), P(), P(), P(), P(), P())
    return jax.shard_map(
        body, mesh=mesh, in_specs=placed, out_specs=P("row", "col", None), check_vma=False
    )
```

```python
import jax
import jax.numpy as jnp
from jax import lax
from jax.experimental.layout import Layout, with_layout_constraint
from jax.sharding import PartitionSpec as P


def layer_norm(values, ln_gain, ln_bias):
    values = values.astype(jnp.float32)
    average = jnp.mean(values, axis=-1, keepdims=True)
    centred = values - average
    variance = jnp.mean(centred * centred, axis=-1, keepdims=True)
    return centred * lax.rsqrt(variance + 1e-05) * ln_gain + ln_bias


def gate_project(normed, keep, weight_proj, weight_gate):
    flat = normed.reshape(-1, normed.shape[-1])
    projected = jnp.dot(flat, weight_proj, preferred_element_type=jnp.float32)
    gate_logit = jnp.dot(flat, weight_gate, preferred_element_type=jnp.float32)
    gated = jax.nn.sigmoid(gate_logit) * projected * keep.astype(jnp.float32).reshape(-1, 1)
    return gated.astype(jnp.bfloat16).reshape(normed.shape[0], normed.shape[1], -1)


def out_gate(normed, w_outgate):
    flat = normed.reshape(-1, normed.shape[-1])
    return jax.nn.sigmoid(jnp.dot(flat, w_outgate, preferred_element_type=jnp.float32))


def spread_of(contracted):
    return contracted, jnp.mean(contracted, axis=0, keepdims=True)


def rescale(contracted, average, out_gain, out_bias):
    centred = contracted - average
    variance = jnp.mean(centred * centred, axis=0, keepdims=True)
    scaled = centred * lax.rsqrt(variance + 1e-05) * out_gain[:, None, None] + out_bias[:, None, None]
    return scaled.astype(jnp.bfloat16)


def finish(current, scaled, gate, w_out):
    branch = jnp.einsum("hij,hc->ijc", scaled, w_out, preferred_element_type=jnp.float32)
    updated = current.astype(jnp.float32) + branch * gate.reshape(branch.shape)
    return updated.astype(jnp.bfloat16)


def swap(x, axis, bits):
    n = lax.axis_size(axis)
    return lax.ppermute(x, axis, [(p, p ^ bits) for p in range(n)])


def put(buffer, x, *at):
    return lax.dynamic_update_slice(buffer, x.reshape((1,) * len(at) + x.shape), at + (0,) * x.ndim)


def gather_col(piece, meanwhile=(), second=lambda x: x):
    col = lax.axis_index("col")
    x, half, core = col // 4, (col // 2) % 2, col % 2
    pair = jnp.zeros((2,) + piece.shape, piece.dtype)
    pair = put(put(pair, piece, half), swap(piece, "col", 2), 1 - half)
    pair, meanwhile = lax.optimization_barrier((pair, meanwhile))
    four = put(jnp.zeros((4,) + pair.shape, piece.dtype), pair, x)
    for d in (2, 1, 3):
        four = put(four, swap(pair, "col", 4 * d), x ^ d)
    four, meanwhile = lax.optimization_barrier((four, second(meanwhile)))
    whole = jnp.zeros((2,) + four.shape, piece.dtype)
    whole = put(put(whole, four, core), swap(four, "col", 1), 1 - core)
    return jnp.moveaxis(whole, 0, 2).reshape((16,) + piece.shape), meanwhile


def transpose_devices(x):
    n = lax.axis_size("row")
    pairs = [(a * n + b, b * n + a) for a in range(n) for b in range(n)]
    return lax.ppermute(x, ("row", "col"), pairs)


def body(
    pair_rep,
    tok_mask,
    windows,
    in_gain,
    in_bias,
    w_proj,
    w_gate,
    out_gain,
    out_bias,
    w_out,
    w_outgate,
):
    tile = pair_rep.shape[0]
    width = pair_rep.shape[2]
    hidden = w_out.shape[1]
    n = lax.axis_size("row")
    part = tile // n
    row_idx = lax.axis_index("row")
    col_idx = lax.axis_index("col")

    def pick(stacked, update):
        return [
            lax.dynamic_index_in_dim(stacked, windows[update, slot], 0, keepdims=False)
            for slot in range(2)
        ]

    def norm_in(values, update):
        return layer_norm(values, in_gain[update], in_bias[update]).astype(jnp.bfloat16)

    def gate_of(normed, update):
        return out_gate(normed, w_outgate[update])

    def scale(made, update):
        return rescale(*made, out_gain[update], out_bias[update])

    keeps = tok_mask.reshape(n, tile)
    row_keep = lax.dynamic_index_in_dim(keeps, row_idx, 0, keepdims=False)
    col_keep = lax.dynamic_index_in_dim(keeps, col_idx, 0, keepdims=False)
    window_keep = [jnp.concatenate(pick(keeps, update)) for update in range(2)]

    pieces = lax.all_to_all(pair_rep.reshape(n, part, tile, width), "col", 0, 0, tiled=True)
    band = jnp.concatenate(pick(pieces, 0), axis=1)
    part_keep = lax.dynamic_slice_in_dim(row_keep, col_idx * part, part)
    gated = gate_project(
        norm_in(band, 0), part_keep[:, None] * window_keep[0][None, :], w_proj[0], w_gate[0]
    )
    left_own, right_own = gated[..., :hidden], gated[..., hidden:]
    right_moved = transpose_devices(right_own)
    left_moved = transpose_devices(left_own)
    source, _ = lax.optimization_barrier((pair_rep, gated))
    gate = gate_of(norm_in(source, 0), 0)
    right_moved, gate = lax.optimization_barrier((right_moved, gate))

    rows = pair_rep.reshape(n, part, tile, width)
    chunks = jnp.concatenate([jnp.broadcast_to(right_moved, (n,) + right_moved.shape), rows], axis=2)
    chunks, left_own = lax.optimization_barrier((chunks, left_own))
    chunks = lax.all_to_all(chunks, "row", 0, 0, tiled=True)
    right = chunks[:, :, : 2 * tile].reshape(tile, 2 * tile, hidden)
    rows = jnp.concatenate(pick(chunks[:, :, 2 * tile :], 1), axis=0)
    lefts, _ = gather_col(jnp.stack([left_own, left_moved]))
    left = lefts[:, 0].reshape(tile, 2 * tile, hidden).transpose(2, 0, 1)
    left = with_layout_constraint(left, Layout(major_to_minor=(0, 1, 2)))
    left_rows = jnp.concatenate(pick(lefts[:, 1], 1), axis=0)

    contracted = jnp.einsum("ikh,jkh->hij", left_rows, right, preferred_element_type=jnp.float32)
    scaled = scale(spread_of(contracted), 0)
    rows = finish(rows, scaled, gate_of(norm_in(rows, 0), 0), w_out[0])
    rows_keep = jnp.concatenate(
        [lax.dynamic_slice_in_dim(k, row_idx * part, part) for k in pick(keeps, 1)]
    )
    gated = gate_project(
        norm_in(rows, 1), rows_keep[:, None] * col_keep[None, :], w_proj[1], w_gate[1]
    )
    next_left = transpose_devices(gated[..., :hidden])
    copies = jnp.broadcast_to(gated[..., hidden:], (n, 2 * part, tile, hidden))
    next_right = lax.all_to_all(copies, "row", 0, 0, tiled=True).reshape(2 * tile, tile, hidden)
    def main_tile(x):
        contracted = jnp.einsum("hik,jkh->hij", x, right, preferred_element_type=jnp.float32)
        return scale(spread_of(contracted), 0)

    next_left, scaled = gather_col(next_left, left, main_tile)
    next_left = next_left.reshape(2 * tile, tile, hidden)
    current = finish(pair_rep, scaled, gate, w_out[0])
    gate = gate_of(norm_in(current, 1), 1)

    contracted = jnp.einsum(
        "kih,kjh->hij", next_left, next_right, preferred_element_type=jnp.float32
    )
    return finish(current, scale(spread_of(contracted), 1), gate, w_out[1])


def solution(mesh):
    placed = (P("row", "col", None), P(), P(), P(), P(), P(), P(), P(), P(), P(), P())
    return jax.shard_map(
        body, mesh=mesh, in_specs=placed, out_specs=P("row", "col", None), check_vma=False
    )
```

```python
import jax
import jax.numpy as jnp
from jax import lax
from jax.experimental.layout import Layout, with_layout_constraint
from jax.sharding import PartitionSpec as P


def layer_norm(values, ln_gain, ln_bias):
    values = values.astype(jnp.float32)
    average = jnp.mean(values, axis=-1, keepdims=True)
    centred = values - average
    variance = jnp.mean(centred * centred, axis=-1, keepdims=True)
    return centred * lax.rsqrt(variance + 1e-05) * ln_gain + ln_bias


def gate_project(normed, keep, weight_proj, weight_gate):
    flat = normed.reshape(-1, normed.shape[-1])
    projected = jnp.dot(flat, weight_proj, preferred_element_type=jnp.float32)
    gate_logit = jnp.dot(flat, weight_gate, preferred_element_type=jnp.float32)
    gated = jax.nn.sigmoid(gate_logit) * projected * keep.astype(jnp.float32).reshape(-1, 1)
    return gated.astype(jnp.bfloat16).reshape(normed.shape[0], normed.shape[1], -1)


def out_gate(normed, w_outgate):
    flat = normed.reshape(-1, normed.shape[-1])
    return jax.nn.sigmoid(jnp.dot(flat, w_outgate, preferred_element_type=jnp.float32))


def spread_of(contracted):
    return contracted, jnp.mean(contracted, axis=0, keepdims=True)


def rescale(contracted, average, out_gain, out_bias):
    centred = contracted - average
    variance = jnp.mean(centred * centred, axis=0, keepdims=True)
    scaled = centred * lax.rsqrt(variance + 1e-05) * out_gain[:, None, None] + out_bias[:, None, None]
    return scaled.astype(jnp.bfloat16)


def finish(current, scaled, gate, w_out):
    branch = jnp.einsum("hij,hc->ijc", scaled, w_out, preferred_element_type=jnp.float32)
    updated = current.astype(jnp.float32) + branch * gate.reshape(branch.shape)
    return updated.astype(jnp.bfloat16)


def swap(x, axis, bits):
    n = lax.axis_size(axis)
    return lax.ppermute(x, axis, [(p, p ^ bits) for p in range(n)])


def put(buffer, x, *at):
    at = at + (jnp.uint32(0),) * x.ndim
    return lax.dynamic_update_slice(buffer, x.reshape((1,) * (len(at) - x.ndim) + x.shape), at)


def gather_col(piece, places, meanwhile=(), second=lambda x: x):
    half, other_half, ring, core, other_core = places
    pair = jnp.zeros((2,) + piece.shape, piece.dtype)
    pair = put(put(pair, piece, half), swap(piece, "col", 2), other_half)
    pair, meanwhile = lax.optimization_barrier((pair, meanwhile))
    four = put(jnp.zeros((4,) + pair.shape, piece.dtype), pair, ring[0])
    for d in (2, 1, 3):
        four = put(four, swap(pair, "col", 4 * d), ring[d])
    four, meanwhile = lax.optimization_barrier((four, second(meanwhile)))
    whole = jnp.zeros((2,) + four.shape, piece.dtype)
    whole = put(put(whole, four, core), swap(four, "col", 1), other_core)
    return jnp.moveaxis(whole, 0, 2).reshape((16,) + piece.shape), meanwhile


def transpose_devices(x):
    n = lax.axis_size("row")
    pairs = [(a * n + b, b * n + a) for a in range(n) for b in range(n)]
    return lax.ppermute(x, ("row", "col"), pairs)


def body(
    pair_rep,
    tok_mask,
    windows,
    in_gain,
    in_bias,
    w_proj,
    w_gate,
    out_gain,
    out_bias,
    w_out,
    w_outgate,
):
    tile = pair_rep.shape[0]
    width = pair_rep.shape[2]
    hidden = w_out.shape[1]
    n = lax.axis_size("row")
    part = tile // n
    row_idx = lax.axis_index("row")
    col_idx = lax.axis_index("col")

    def pick(stacked, update):
        return [
            lax.dynamic_index_in_dim(stacked, windows[update, slot], 0, keepdims=False)
            for slot in range(2)
        ]

    def norm_in(values, update):
        return layer_norm(values, in_gain[update], in_bias[update]).astype(jnp.bfloat16)

    def gate_of(normed, update):
        return out_gate(normed, w_outgate[update])

    def scale(made, update):
        return rescale(*made, out_gain[update], out_bias[update])

    def keep_of(start, count):
        return lax.dynamic_slice_in_dim(tok_mask, start, count, allow_negative_indices=False)

    part_keep = keep_of(row_idx * tile + col_idx * part, part)
    col_keep = keep_of(col_idx * tile, tile)
    window_keep = jnp.concatenate([keep_of(windows[0, slot] * tile, tile) for slot in range(2)])
    rows_keep = jnp.concatenate(
        [keep_of(windows[1, slot] * tile + row_idx * part, part) for slot in range(2)]
    )
    col = col_idx.astype(jnp.uint32)
    half, core = (col >> 1) & 1, col & 1
    places = (half, half ^ 1, [(col >> 2) ^ d for d in range(4)], core, core ^ 1)

    pieces = lax.all_to_all(pair_rep.reshape(n, part, tile, width), "col", 0, 0, tiled=True)
    gate = gate_of(norm_in(pair_rep, 0), 0)
    pieces, places, gate = lax.optimization_barrier((pieces, places, gate))
    band = jnp.concatenate(pick(pieces, 0), axis=1)
    gated = gate_project(
        norm_in(band, 0), part_keep[:, None] * window_keep[None, :], w_proj[0], w_gate[0]
    )
    left_own, right_own = gated[..., :hidden], gated[..., hidden:]
    right_moved = transpose_devices(right_own)
    left_moved = transpose_devices(left_own)

    rows = pair_rep.reshape(n, part, tile, width)
    chunks = jnp.concatenate([jnp.broadcast_to(right_moved, (n,) + right_moved.shape), rows], axis=2)
    chunks, left_own = lax.optimization_barrier((chunks, left_own))
    chunks = lax.all_to_all(chunks, "row", 0, 0, tiled=True)
    right = chunks[:, :, : 2 * tile].reshape(tile, 2 * tile, hidden)
    rows = jnp.concatenate(pick(chunks[:, :, 2 * tile :], 1), axis=0)
    lefts, _ = gather_col(jnp.stack([left_own, left_moved]), places)
    left = lefts[:, 0].reshape(tile, 2 * tile, hidden)
    left_rows = jnp.concatenate(pick(lefts[:, 1], 1), axis=0)

    contracted = jnp.einsum("ikh,jkh->hij", left_rows, right, preferred_element_type=jnp.float32)
    scaled = scale(spread_of(contracted), 0)
    rows = finish(rows, scaled, gate_of(norm_in(rows, 0), 0), w_out[0])
    gated = gate_project(
        norm_in(rows, 1), rows_keep[:, None] * col_keep[None, :], w_proj[1], w_gate[1]
    )
    next_left = transpose_devices(gated[..., :hidden])
    copies = jnp.broadcast_to(gated[..., hidden:], (n, 2 * part, tile, hidden))
    next_right = lax.all_to_all(copies, "row", 0, 0, tiled=True).reshape(2 * tile, tile, hidden)

    def main_tile(x):
        contracted = jnp.einsum("hik,jkh->hij", x, right, preferred_element_type=jnp.float32)
        return scale(spread_of(contracted), 0)

    next_left, left = lax.optimization_barrier((next_left, left))
    left = with_layout_constraint(left.transpose(2, 0, 1), Layout(major_to_minor=(0, 1, 2)))
    next_left, scaled = gather_col(next_left, places, left, main_tile)
    next_left = next_left.reshape(2 * tile, tile, hidden)
    current = finish(pair_rep, scaled, gate, w_out[0])
    gate = gate_of(norm_in(current, 1), 1)

    contracted = jnp.einsum(
        "kih,kjh->hij", next_left, next_right, preferred_element_type=jnp.float32
    )
    return finish(current, scale(spread_of(contracted), 1), gate, w_out[1])


def solution(mesh):
    placed = (P("row", "col", None), P(), P(), P(), P(), P(), P(), P(), P(), P(), P())
    return jax.shard_map(
        body, mesh=mesh, in_specs=placed, out_specs=P("row", "col", None), check_vma=False
    )
```

```python
import jax
import jax.numpy as jnp
from jax import lax
from jax.experimental.layout import Layout, with_layout_constraint
from jax.sharding import PartitionSpec as P


def layer_norm(values, ln_gain, ln_bias):
    values = values.astype(jnp.float32)
    average = jnp.mean(values, axis=-1, keepdims=True)
    centred = values - average
    variance = jnp.mean(centred * centred, axis=-1, keepdims=True)
    return centred * lax.rsqrt(variance + 1e-05) * ln_gain + ln_bias


def gate_project(normed, keep, weight_proj, weight_gate):
    flat = normed.reshape(-1, normed.shape[-1])
    projected = jnp.dot(flat, weight_proj, preferred_element_type=jnp.float32)
    gate_logit = jnp.dot(flat, weight_gate, preferred_element_type=jnp.float32)
    gated = jax.nn.sigmoid(gate_logit) * projected * keep[:, None]
    return gated.astype(jnp.bfloat16).reshape(normed.shape[0], normed.shape[1], -1)


def out_gate(normed, w_outgate):
    flat = normed.reshape(-1, normed.shape[-1])
    return jax.nn.sigmoid(jnp.dot(flat, w_outgate, preferred_element_type=jnp.float32))


def spread_of(contracted):
    return contracted, jnp.mean(contracted, axis=0, keepdims=True)


def rescale(contracted, average, out_gain, out_bias):
    centred = contracted - average
    variance = jnp.mean(centred * centred, axis=0, keepdims=True)
    scaled = centred * lax.rsqrt(variance + 1e-05) * out_gain[:, None, None] + out_bias[:, None, None]
    return scaled.astype(jnp.bfloat16)


def finish(current, scaled, gate, w_out):
    branch = jnp.einsum("hij,hc->ijc", scaled, w_out, preferred_element_type=jnp.float32)
    updated = current.astype(jnp.float32) + branch * gate.reshape(branch.shape)
    return updated.astype(jnp.bfloat16)


def swap(x, axis, bits):
    n = lax.axis_size(axis)
    return lax.ppermute(x, axis, [(p, p ^ bits) for p in range(n)])


def put(buffer, x, *at):
    at = at + (jnp.uint32(0),) * x.ndim
    return lax.dynamic_update_slice(buffer, x.reshape((1,) * (len(at) - x.ndim) + x.shape), at)


def gather_col(piece, places, meanwhile=(), second=lambda x: x):
    half, other_half, ring, core, other_core = places
    pair = jnp.zeros((2,) + piece.shape, piece.dtype)
    pair = put(put(pair, piece, half), swap(piece, "col", 2), other_half)
    pair, meanwhile = lax.optimization_barrier((pair, meanwhile))
    four = put(jnp.zeros((4,) + pair.shape, piece.dtype), pair, ring[0])
    for d in (2, 1, 3):
        four = put(four, swap(pair, "col", 4 * d), ring[d])
    four, meanwhile = lax.optimization_barrier((four, second(meanwhile)))
    whole = jnp.zeros((2,) + four.shape, piece.dtype)
    whole = put(put(whole, four, core), swap(four, "col", 1), other_core)
    return jnp.moveaxis(whole, 0, 2).reshape((16,) + piece.shape), meanwhile


def transpose_devices(x):
    n = lax.axis_size("row")
    pairs = [(a * n + b, b * n + a) for a in range(n) for b in range(n)]
    return lax.ppermute(x, ("row", "col"), pairs)


def body(
    pair_rep,
    tok_mask,
    windows,
    in_gain,
    in_bias,
    w_proj,
    w_gate,
    out_gain,
    out_bias,
    w_out,
    w_outgate,
):
    tile = pair_rep.shape[0]
    width = pair_rep.shape[2]
    hidden = w_out.shape[1]
    n = lax.axis_size("row")
    part = tile // n
    row_idx = lax.axis_index("row")
    col_idx = lax.axis_index("col")

    def pick(stacked, update):
        return [
            lax.dynamic_index_in_dim(stacked, windows[update, slot], 0, keepdims=False)
            for slot in range(2)
        ]

    def norm_in(values, update):
        return layer_norm(values, in_gain[update], in_bias[update]).astype(jnp.bfloat16)

    def gate_of(normed, update):
        return out_gate(normed, w_outgate[update])

    def scale(made, update):
        return rescale(*made, out_gain[update], out_bias[update])

    row = row_idx.astype(jnp.uint32)
    col = col_idx.astype(jnp.uint32)
    zero = jnp.uint32(0)
    keeps = tok_mask.astype(jnp.float32).reshape(n, tile)

    def keep_of(block):
        return lax.dynamic_slice(keeps, (block.astype(jnp.uint32), zero), (1, tile))[0]

    def part_of(keep, place):
        return lax.dynamic_slice(keep, (place * part,), (part,))

    window_keep = jnp.concatenate([keep_of(windows[0, slot]) for slot in range(2)])
    rows_keep = jnp.concatenate([part_of(keep_of(windows[1, slot]), row) for slot in range(2)])
    band_keep = (part_of(keep_of(row), col)[:, None] * window_keep[None, :]).reshape(-1)
    rows_keep = (rows_keep[:, None] * keep_of(col)[None, :]).reshape(-1)
    half, core = (col >> 1) & 1, col & 1
    places = (half, half ^ 1, [(col >> 2) ^ d for d in range(4)], core, core ^ 1)

    pieces = lax.all_to_all(pair_rep.reshape(n, part, tile, width), "col", 0, 0, tiled=True)
    gate = gate_of(norm_in(pair_rep, 0), 0)
    pieces, places, gate, band_keep, rows_keep = lax.optimization_barrier(
        (pieces, places, gate, band_keep, rows_keep)
    )
    band = jnp.concatenate(pick(pieces, 0), axis=1)
    gated = gate_project(norm_in(band, 0), band_keep, w_proj[0], w_gate[0])
    left_own, right_own = gated[..., :hidden], gated[..., hidden:]
    right_moved = transpose_devices(right_own)
    left_moved = transpose_devices(left_own)

    rows = pair_rep.reshape(n, part, tile, width)
    chunks = jnp.concatenate([jnp.broadcast_to(right_moved, (n,) + right_moved.shape), rows], axis=2)
    chunks, left_own = lax.optimization_barrier((chunks, left_own))
    chunks = lax.all_to_all(chunks, "row", 0, 0, tiled=True)
    rows = jnp.concatenate(pick(chunks[:, :, 2 * tile :], 1), axis=0)
    chunks, rows = lax.optimization_barrier((chunks, rows))
    right = chunks[:, :, : 2 * tile].reshape(tile, 2 * tile, hidden)
    lefts, _ = gather_col(jnp.stack([left_own, left_moved]), places)
    left = lefts[:, 0].reshape(tile, 2 * tile, hidden)
    left_rows = jnp.concatenate(pick(lefts[:, 1], 1), axis=0)

    contracted = jnp.einsum("ikh,jkh->hij", left_rows, right, preferred_element_type=jnp.float32)
    scaled = scale(spread_of(contracted), 0)
    rows = finish(rows, scaled, gate_of(norm_in(rows, 0), 0), w_out[0])
    gated = gate_project(norm_in(rows, 1), rows_keep, w_proj[1], w_gate[1])
    next_left = transpose_devices(gated[..., :hidden])
    copies = jnp.broadcast_to(gated[..., hidden:], (n, 2 * part, tile, hidden))
    next_right = lax.all_to_all(copies, "row", 0, 0, tiled=True).reshape(2 * tile, tile, hidden)

    def main_tile(x):
        contracted = jnp.einsum("hik,jkh->hij", x, right, preferred_element_type=jnp.float32)
        return scale(spread_of(contracted), 0)

    next_left, left = lax.optimization_barrier((next_left, left))
    left = with_layout_constraint(left.transpose(2, 0, 1), Layout(major_to_minor=(0, 1, 2)))
    next_left, scaled = gather_col(next_left, places, left, main_tile)
    next_left = next_left.reshape(2 * tile, tile, hidden)
    current = finish(pair_rep, scaled, gate, w_out[0])
    gate = gate_of(norm_in(current, 1), 1)

    contracted = jnp.einsum(
        "kih,kjh->hij", next_left, next_right, preferred_element_type=jnp.float32
    )
    return finish(current, scale(spread_of(contracted), 1), gate, w_out[1])


def solution(mesh):
    placed = (P("row", "col", None), P(), P(), P(), P(), P(), P(), P(), P(), P(), P())
    return jax.shard_map(
        body, mesh=mesh, in_specs=placed, out_specs=P("row", "col", None), check_vma=False
    )
```

```python
import jax
import jax.numpy as jnp
from jax import lax
from jax.experimental.layout import Layout, with_layout_constraint
from jax.sharding import PartitionSpec as P


def layer_norm(values, ln_gain, ln_bias):
    values = values.astype(jnp.float32)
    average = jnp.mean(values, axis=-1, keepdims=True)
    centred = values - average
    variance = jnp.mean(centred * centred, axis=-1, keepdims=True)
    return centred * lax.rsqrt(variance + 1e-05) * ln_gain + ln_bias


def gate_project(normed, keep, weight_proj, weight_gate):
    flat = normed.reshape(-1, normed.shape[-1])
    projected = jnp.dot(flat, weight_proj, preferred_element_type=jnp.float32)
    gate_logit = jnp.dot(flat, weight_gate, preferred_element_type=jnp.float32)
    gated = jax.nn.sigmoid(gate_logit) * projected * keep[:, None]
    return gated.astype(jnp.bfloat16).reshape(normed.shape[0], normed.shape[1], -1)


def out_gate(normed, w_outgate):
    flat = normed.reshape(-1, normed.shape[-1])
    return jax.nn.sigmoid(jnp.dot(flat, w_outgate, preferred_element_type=jnp.float32))


def spread_of(contracted):
    return contracted, jnp.mean(contracted, axis=0, keepdims=True)


def rescale(contracted, average, out_gain, out_bias):
    centred = contracted - average
    variance = jnp.mean(centred * centred, axis=0, keepdims=True)
    scaled = centred * lax.rsqrt(variance + 1e-05) * out_gain[:, None, None] + out_bias[:, None, None]
    return scaled.astype(jnp.bfloat16)


def finish(current, scaled, gate, w_out):
    branch = jnp.einsum("hij,hc->ijc", scaled, w_out, preferred_element_type=jnp.float32)
    updated = current.astype(jnp.float32) + branch * gate.reshape(branch.shape)
    return updated.astype(jnp.bfloat16)


def swap(x, axis, bits):
    n = lax.axis_size(axis)
    return lax.ppermute(x, axis, [(p, p ^ bits) for p in range(n)])


def put(buffer, x, *at):
    at = at + (jnp.uint32(0),) * x.ndim
    return lax.dynamic_update_slice(buffer, x.reshape((1,) * (len(at) - x.ndim) + x.shape), at)


def gather_col(piece, places, meanwhile=(), second=lambda x: x):
    half, other_half, ring, core, other_core = places
    pair = jnp.zeros((2,) + piece.shape, piece.dtype)
    pair = put(put(pair, piece, half), swap(piece, "col", 2), other_half)
    pair, meanwhile = lax.optimization_barrier((pair, meanwhile))
    four = put(jnp.zeros((4,) + pair.shape, piece.dtype), pair, ring[0])
    for d in (2, 1, 3):
        four = put(four, swap(pair, "col", 4 * d), ring[d])
    four, meanwhile = lax.optimization_barrier((four, second(meanwhile)))
    whole = jnp.zeros((2,) + four.shape, piece.dtype)
    whole = put(put(whole, four, core), swap(four, "col", 1), other_core)
    return jnp.moveaxis(whole, 0, 2).reshape((16,) + piece.shape), meanwhile


def transpose_devices(x):
    n = lax.axis_size("row")
    pairs = [(a * n + b, b * n + a) for a in range(n) for b in range(n)]
    return lax.ppermute(x, ("row", "col"), pairs)


def body(
    pair_rep,
    tok_mask,
    windows,
    in_gain,
    in_bias,
    w_proj,
    w_gate,
    out_gain,
    out_bias,
    w_out,
    w_outgate,
):
    tile = pair_rep.shape[0]
    width = pair_rep.shape[2]
    hidden = w_out.shape[1]
    n = lax.axis_size("row")
    part = tile // n
    row_idx = lax.axis_index("row")
    col_idx = lax.axis_index("col")

    def pick(stacked, update):
        return [
            lax.dynamic_index_in_dim(stacked, windows[update, slot], 0, keepdims=False)
            for slot in range(2)
        ]

    def norm_in(values, update):
        return layer_norm(values, in_gain[update], in_bias[update]).astype(jnp.bfloat16)

    def gate_of(normed, update):
        return out_gate(normed, w_outgate[update])

    def scale(made, update):
        return rescale(*made, out_gain[update], out_bias[update])

    row = row_idx.astype(jnp.uint32)
    col = col_idx.astype(jnp.uint32)
    zero = jnp.uint32(0)
    keeps = tok_mask.astype(jnp.float32).reshape(n, tile)

    def keep_of(block):
        return lax.dynamic_slice(keeps, (block.astype(jnp.uint32), zero), (1, tile))[0]

    def part_of(keep, place):
        return lax.dynamic_slice(keep, (place * part,), (part,))

    window_keep = jnp.concatenate([keep_of(windows[0, slot]) for slot in range(2)])
    rows_keep = jnp.concatenate([part_of(keep_of(windows[1, slot]), row) for slot in range(2)])
    band_keep = (part_of(keep_of(row), col)[:, None] * window_keep[None, :]).reshape(-1)
    rows_keep = (rows_keep[:, None] * keep_of(col)[None, :]).reshape(-1)
    half, core = (col >> 1) & 1, col & 1
    places = (half, half ^ 1, [(col >> 2) ^ d for d in range(4)], core, core ^ 1)

    pieces = lax.all_to_all(pair_rep.reshape(n, part, tile, width), "col", 0, 0, tiled=True)
    pieces, places, band_keep, rows_keep = lax.optimization_barrier(
        (pieces, places, band_keep, rows_keep)
    )
    band = jnp.concatenate(pick(pieces, 0), axis=1)
    gated = gate_project(norm_in(band, 0), band_keep, w_proj[0], w_gate[0])
    left_own, right_own = gated[..., :hidden], gated[..., hidden:]
    right_moved = transpose_devices(right_own)
    left_moved = transpose_devices(left_own)
    source, _ = lax.optimization_barrier((pair_rep, right_own))
    gate = gate_of(norm_in(source, 0), 0)
    right_moved, gate = lax.optimization_barrier((right_moved, gate))

    rows = pair_rep.reshape(n, part, tile, width)
    chunks = jnp.concatenate([jnp.broadcast_to(right_moved, (n,) + right_moved.shape), rows], axis=2)
    chunks, left_own = lax.optimization_barrier((chunks, left_own))
    chunks = lax.all_to_all(chunks, "row", 0, 0, tiled=True)
    rows = jnp.concatenate(pick(chunks[:, :, 2 * tile :], 1), axis=0)
    chunks, rows = lax.optimization_barrier((chunks, rows))
    right = chunks[:, :, : 2 * tile].reshape(tile, 2 * tile, hidden)
    lefts, _ = gather_col(jnp.stack([left_own, left_moved]), places)
    left = lefts[:, 0].reshape(tile, 2 * tile, hidden)
    left_rows = jnp.concatenate(pick(lefts[:, 1], 1), axis=0)

    contracted = jnp.einsum("ikh,jkh->hij", left_rows, right, preferred_element_type=jnp.float32)
    scaled = scale(spread_of(contracted), 0)
    rows = finish(rows, scaled, gate_of(norm_in(rows, 0), 0), w_out[0])
    gated = gate_project(norm_in(rows, 1), rows_keep, w_proj[1], w_gate[1])
    next_left = transpose_devices(gated[..., :hidden])
    copies = jnp.broadcast_to(gated[..., hidden:], (n, 2 * part, tile, hidden))
    next_right = lax.all_to_all(copies, "row", 0, 0, tiled=True).reshape(2 * tile, tile, hidden)

    def main_tile(x):
        contracted = jnp.einsum("hik,jkh->hij", x, right, preferred_element_type=jnp.float32)
        return scale(spread_of(contracted), 0)

    next_left, left = lax.optimization_barrier((next_left, left))
    left = with_layout_constraint(left.transpose(2, 0, 1), Layout(major_to_minor=(0, 1, 2)))
    next_left, scaled = gather_col(next_left, places, left, main_tile)
    next_left = next_left.reshape(2 * tile, tile, hidden)
    current = finish(pair_rep, scaled, gate, w_out[0])
    gate = gate_of(norm_in(current, 1), 1)

    contracted = jnp.einsum(
        "kih,kjh->hij", next_left, next_right, preferred_element_type=jnp.float32
    )
    return finish(current, scale(spread_of(contracted), 1), gate, w_out[1])


def solution(mesh):
    placed = (P("row", "col", None), P(), P(), P(), P(), P(), P(), P(), P(), P(), P())
    return jax.shard_map(
        body, mesh=mesh, in_specs=placed, out_specs=P("row", "col", None), check_vma=False
    )
```

```python
import jax
import jax.numpy as jnp
from jax import lax
from jax.experimental.layout import Layout, with_layout_constraint
from jax.sharding import PartitionSpec as P


def layer_norm(values, ln_gain, ln_bias):
    values = values.astype(jnp.float32)
    average = jnp.mean(values, axis=-1, keepdims=True)
    centred = values - average
    variance = jnp.mean(centred * centred, axis=-1, keepdims=True)
    return centred * lax.rsqrt(variance + 1e-05) * ln_gain + ln_bias


def gate_project(normed, keep, weight_proj, weight_gate):
    flat = normed.reshape(-1, normed.shape[-1])
    projected = jnp.dot(flat, weight_proj, preferred_element_type=jnp.float32)
    gate_logit = jnp.dot(flat, weight_gate, preferred_element_type=jnp.float32)
    gated = jax.nn.sigmoid(gate_logit) * projected * keep[:, None]
    return gated.astype(jnp.bfloat16).reshape(normed.shape[0], normed.shape[1], -1)


def out_gate(normed, w_outgate):
    flat = normed.reshape(-1, normed.shape[-1])
    return jax.nn.sigmoid(jnp.dot(flat, w_outgate, preferred_element_type=jnp.float32))


def spread_of(contracted):
    return contracted, jnp.mean(contracted, axis=0, keepdims=True)


def rescale(contracted, average, out_gain, out_bias):
    centred = contracted - average
    variance = jnp.mean(centred * centred, axis=0, keepdims=True)
    scaled = centred * lax.rsqrt(variance + 1e-05) * out_gain[:, None, None] + out_bias[:, None, None]
    return scaled.astype(jnp.bfloat16)


def finish(current, scaled, gate, w_out):
    branch = jnp.einsum("hij,hc->ijc", scaled, w_out, preferred_element_type=jnp.float32)
    updated = current.astype(jnp.float32) + branch * gate.reshape(branch.shape)
    return updated.astype(jnp.bfloat16)


def swap(x, axis, bits):
    n = lax.axis_size(axis)
    return lax.ppermute(x, axis, [(p, p ^ bits) for p in range(n)])


def put(buffer, x, *at):
    at = at + (jnp.uint32(0),) * x.ndim
    return lax.dynamic_update_slice(buffer, x.reshape((1,) * (len(at) - x.ndim) + x.shape), at)


def gather_col(piece, places, meanwhile=(), second=lambda x: x):
    half, other_half, ring, core, other_core = places
    pair = jnp.zeros((2,) + piece.shape, piece.dtype)
    pair = put(put(pair, piece, half), swap(piece, "col", 2), other_half)
    pair, meanwhile = lax.optimization_barrier((pair, meanwhile))
    four = put(jnp.zeros((4,) + pair.shape, piece.dtype), pair, ring[0])
    for d in (2, 1, 3):
        four = put(four, swap(pair, "col", 4 * d), ring[d])
    four, meanwhile = lax.optimization_barrier((four, second(meanwhile)))
    whole = jnp.zeros((2,) + four.shape, piece.dtype)
    whole = put(put(whole, four, core), swap(four, "col", 1), other_core)
    return jnp.moveaxis(whole, 0, 2).reshape((16,) + piece.shape), meanwhile


def transpose_devices(x):
    n = lax.axis_size("row")
    pairs = [(a * n + b, b * n + a) for a in range(n) for b in range(n)]
    return lax.ppermute(x, ("row", "col"), pairs)


def body(
    pair_rep,
    tok_mask,
    windows,
    in_gain,
    in_bias,
    w_proj,
    w_gate,
    out_gain,
    out_bias,
    w_out,
    w_outgate,
):
    tile = pair_rep.shape[0]
    width = pair_rep.shape[2]
    hidden = w_out.shape[1]
    n = lax.axis_size("row")
    part = tile // n
    row_idx = lax.axis_index("row")
    col_idx = lax.axis_index("col")

    def pick(stacked, update):
        return [
            lax.dynamic_index_in_dim(stacked, windows[update, slot], 0, keepdims=False)
            for slot in range(2)
        ]

    def norm_in(values, update):
        return layer_norm(values, in_gain[update], in_bias[update]).astype(jnp.bfloat16)

    def gate_of(normed, update):
        return out_gate(normed, w_outgate[update])

    def scale(made, update):
        return rescale(*made, out_gain[update], out_bias[update])

    row = row_idx.astype(jnp.uint32)
    col = col_idx.astype(jnp.uint32)
    zero = jnp.uint32(0)
    keeps = tok_mask.astype(jnp.float32).reshape(n, tile)

    def keep_of(block):
        return lax.dynamic_slice(keeps, (block.astype(jnp.uint32), zero), (1, tile))[0]

    def part_of(keep, place):
        return lax.dynamic_slice(keep, (place * part,), (part,))

    window_keep = jnp.concatenate([keep_of(windows[0, slot]) for slot in range(2)])
    rows_keep = jnp.concatenate([part_of(keep_of(windows[1, slot]), row) for slot in range(2)])
    band_keep = (part_of(keep_of(row), col)[:, None] * window_keep[None, :]).reshape(-1)
    rows_keep = (rows_keep[:, None] * keep_of(col)[None, :]).reshape(-1)
    half, core = (col >> 1) & 1, col & 1
    places = (half, half ^ 1, [(col >> 2) ^ d for d in range(4)], core, core ^ 1)

    pieces = lax.all_to_all(pair_rep.reshape(n, part, tile, width), "col", 0, 0, tiled=True)
    pieces, places, band_keep, rows_keep = lax.optimization_barrier(
        (pieces, places, band_keep, rows_keep)
    )
    band = jnp.concatenate(pick(pieces, 0), axis=1)
    gated = gate_project(norm_in(band, 0), band_keep, w_proj[0], w_gate[0])
    left_own, right_own = gated[..., :hidden], gated[..., hidden:]
    right_moved = transpose_devices(right_own)
    left_moved = transpose_devices(left_own)
    source, _ = lax.optimization_barrier((pair_rep, right_own))
    gate = gate_of(norm_in(source, 0), 0)
    right_moved, gate = lax.optimization_barrier((right_moved, gate))

    rows = pair_rep.reshape(n, part, tile, width)
    chunks = jnp.concatenate([jnp.broadcast_to(right_moved, (n,) + right_moved.shape), rows], axis=2)
    chunks, left_own = lax.optimization_barrier((chunks, left_own))
    chunks = lax.all_to_all(chunks, "row", 0, 0, tiled=True)
    rows = pick(chunks[:, :, 2 * tile :], 1)
    chunks, rows = lax.optimization_barrier((chunks, rows))
    rows = jnp.concatenate(rows, axis=0)
    right = chunks[:, :, : 2 * tile].reshape(tile, 2 * tile, hidden)
    lefts, _ = gather_col(jnp.stack([left_own, left_moved]), places)
    left = lefts[:, 0].reshape(tile, 2 * tile, hidden)
    left_rows = jnp.concatenate(pick(lefts[:, 1], 1), axis=0)

    contracted = jnp.einsum("ikh,jkh->hij", left_rows, right, preferred_element_type=jnp.float32)
    scaled = scale(spread_of(contracted), 0)
    rows = finish(rows, scaled, gate_of(norm_in(rows, 0), 0), w_out[0])
    gated = gate_project(norm_in(rows, 1), rows_keep, w_proj[1], w_gate[1])
    next_left = transpose_devices(gated[..., :hidden])
    copies = jnp.broadcast_to(gated[..., hidden:], (n, 2 * part, tile, hidden))
    next_right = lax.all_to_all(copies, "row", 0, 0, tiled=True).reshape(2 * tile, tile, hidden)

    def main_tile(x):
        contracted = jnp.einsum("hik,jkh->hij", x, right, preferred_element_type=jnp.float32)
        return scale(spread_of(contracted), 0)

    next_left, left = lax.optimization_barrier((next_left, left))
    left = with_layout_constraint(left.transpose(2, 0, 1), Layout(major_to_minor=(0, 1, 2)))
    next_left, scaled = gather_col(next_left, places, left, main_tile)
    next_left = next_left.reshape(2 * tile, tile, hidden)
    current = finish(pair_rep, scaled, gate, w_out[0])
    gate = gate_of(norm_in(current, 1), 1).reshape(current.shape)
    kept = lax.optimization_barrier(jnp.stack([gate, current.astype(jnp.float32)]))

    contracted = jnp.einsum(
        "kih,kjh->hij", next_left, next_right, preferred_element_type=jnp.float32
    )
    return finish(kept[1], scale(spread_of(contracted), 1), kept[0], w_out[1])


def solution(mesh):
    placed = (P("row", "col", None), P(), P(), P(), P(), P(), P(), P(), P(), P(), P())
    return jax.shard_map(
        body, mesh=mesh, in_specs=placed, out_specs=P("row", "col", None), check_vma=False
    )
```

```python
import jax
import jax.numpy as jnp
from jax import lax
from jax.experimental.layout import Layout, with_layout_constraint
from jax.sharding import PartitionSpec as P


def layer_norm(values, ln_gain, ln_bias):
    values = values.astype(jnp.float32)
    average = jnp.mean(values, axis=-1, keepdims=True)
    centred = values - average
    variance = jnp.mean(centred * centred, axis=-1, keepdims=True)
    return centred * lax.rsqrt(variance + 1e-05) * ln_gain + ln_bias


def gate_project(normed, keep, weight_proj, weight_gate):
    flat = normed.reshape(-1, normed.shape[-1])
    projected = jnp.dot(flat, weight_proj, preferred_element_type=jnp.float32)
    gate_logit = jnp.dot(flat, weight_gate, preferred_element_type=jnp.float32)
    gated = jax.nn.sigmoid(gate_logit) * projected * keep[:, None]
    return gated.astype(jnp.bfloat16).reshape(normed.shape[0], normed.shape[1], -1)


def out_gate(normed, w_outgate):
    flat = normed.reshape(-1, normed.shape[-1])
    return jax.nn.sigmoid(jnp.dot(flat, w_outgate, preferred_element_type=jnp.float32))


def spread_of(contracted):
    return contracted, jnp.mean(contracted, axis=0, keepdims=True)


def rescale(contracted, average, out_gain, out_bias):
    centred = contracted - average
    variance = jnp.mean(centred * centred, axis=0, keepdims=True)
    scaled = centred * lax.rsqrt(variance + 1e-05) * out_gain[:, None, None] + out_bias[:, None, None]
    return scaled.astype(jnp.bfloat16)


def finish(current, scaled, gate, w_out):
    branch = jnp.einsum("hij,hc->ijc", scaled, w_out, preferred_element_type=jnp.float32)
    updated = current.astype(jnp.float32) + branch * gate.reshape(branch.shape)
    return updated.astype(jnp.bfloat16)


def swap(x, axis, bits):
    n = lax.axis_size(axis)
    return lax.ppermute(x, axis, [(p, p ^ bits) for p in range(n)])


def put(buffer, x, *at):
    at = at + (jnp.uint32(0),) * x.ndim
    return lax.dynamic_update_slice(buffer, x.reshape((1,) * (len(at) - x.ndim) + x.shape), at)


def gather_col(piece, places, meanwhile=(), second=lambda x: x):
    half, other_half, ring, core, other_core = places
    pair = jnp.zeros((2,) + piece.shape, piece.dtype)
    pair = put(put(pair, piece, half), swap(piece, "col", 2), other_half)
    pair, meanwhile = lax.optimization_barrier((pair, meanwhile))
    four = put(jnp.zeros((4,) + pair.shape, piece.dtype), pair, ring[0])
    for d in (2, 1, 3):
        four = put(four, swap(pair, "col", 4 * d), ring[d])
    four, meanwhile = lax.optimization_barrier((four, second(meanwhile)))
    whole = jnp.zeros((2,) + four.shape, piece.dtype)
    whole = put(put(whole, four, core), swap(four, "col", 1), other_core)
    return jnp.moveaxis(whole, 0, 2).reshape((16,) + piece.shape), meanwhile


def transpose_devices(x):
    n = lax.axis_size("row")
    pairs = [(a * n + b, b * n + a) for a in range(n) for b in range(n)]
    return lax.ppermute(x, ("row", "col"), pairs)


def body(
    pair_rep,
    tok_mask,
    windows,
    in_gain,
    in_bias,
    w_proj,
    w_gate,
    out_gain,
    out_bias,
    w_out,
    w_outgate,
):
    tile = pair_rep.shape[0]
    width = pair_rep.shape[2]
    hidden = w_out.shape[1]
    n = lax.axis_size("row")
    part = tile // n
    row_idx = lax.axis_index("row")
    col_idx = lax.axis_index("col")

    def pick(stacked, update):
        return [
            lax.dynamic_index_in_dim(stacked, windows[update, slot], 0, keepdims=False)
            for slot in range(2)
        ]

    def norm_in(values, update):
        return layer_norm(values, in_gain[update], in_bias[update]).astype(jnp.bfloat16)

    def gate_of(normed, update):
        return out_gate(normed, w_outgate[update])

    def scale(made, update):
        return rescale(*made, out_gain[update], out_bias[update])

    row = row_idx.astype(jnp.uint32)
    col = col_idx.astype(jnp.uint32)
    zero = jnp.uint32(0)
    keeps = tok_mask.astype(jnp.float32).reshape(n, tile)

    def keep_of(block):
        return lax.dynamic_slice(keeps, (block.astype(jnp.uint32), zero), (1, tile))[0]

    def part_of(keep, place):
        return lax.dynamic_slice(keep, (place * part,), (part,))

    window_keep = jnp.concatenate([keep_of(windows[0, slot]) for slot in range(2)])
    rows_keep = jnp.concatenate([part_of(keep_of(windows[1, slot]), row) for slot in range(2)])
    band_keep = (part_of(keep_of(row), col)[:, None] * window_keep[None, :]).reshape(-1)
    moved_keep = (part_of(keep_of(col), row)[:, None] * window_keep[None, :]).reshape(-1)
    rows_keep = (rows_keep[:, None] * keep_of(col)[None, :]).reshape(-1)
    half, core = (col >> 1) & 1, col & 1
    places = (half, half ^ 1, [(col >> 2) ^ d for d in range(4)], core, core ^ 1)

    pieces = lax.all_to_all(pair_rep.reshape(n, part, tile, width), "col", 0, 0, tiled=True)
    pieces, places, band_keep, moved_keep, rows_keep = lax.optimization_barrier(
        (pieces, places, band_keep, moved_keep, rows_keep)
    )
    band = jnp.concatenate(pick(pieces, 0), axis=1)
    band = norm_in(band, 0)
    moved = transpose_devices(band)
    source, band = lax.optimization_barrier((pair_rep, band))
    gate = gate_of(norm_in(source, 0), 0)
    left_own = gate_project(band, band_keep, w_proj[0][:, :hidden], w_gate[0][:, :hidden])
    moved, gate, left_own = lax.optimization_barrier((moved, gate, left_own))
    gated = gate_project(moved, moved_keep, w_proj[0], w_gate[0])
    left_moved, right_moved = gated[..., :hidden], gated[..., hidden:]

    rows = pair_rep.reshape(n, part, tile, width)
    chunks = jnp.concatenate([jnp.broadcast_to(right_moved, (n,) + right_moved.shape), rows], axis=2)
    chunks, left_own = lax.optimization_barrier((chunks, left_own))
    chunks = lax.all_to_all(chunks, "row", 0, 0, tiled=True)
    rows = pick(chunks[:, :, 2 * tile :], 1)
    chunks, rows = lax.optimization_barrier((chunks, rows))
    rows = jnp.concatenate(rows, axis=0)
    right = chunks[:, :, : 2 * tile].reshape(tile, 2 * tile, hidden)
    lefts, _ = gather_col(jnp.stack([left_own, left_moved]), places)
    left = lefts[:, 0].reshape(tile, 2 * tile, hidden)
    left_rows = jnp.concatenate(pick(lefts[:, 1], 1), axis=0)

    contracted = jnp.einsum("ikh,jkh->hij", left_rows, right, preferred_element_type=jnp.float32)
    scaled = scale(spread_of(contracted), 0)
    rows = finish(rows, scaled, gate_of(norm_in(rows, 0), 0), w_out[0])
    gated = gate_project(norm_in(rows, 1), rows_keep, w_proj[1], w_gate[1])
    next_left = transpose_devices(gated[..., :hidden])
    copies = jnp.broadcast_to(gated[..., hidden:], (n, 2 * part, tile, hidden))
    next_right = lax.all_to_all(copies, "row", 0, 0, tiled=True).reshape(2 * tile, tile, hidden)

    def main_tile(x):
        contracted = jnp.einsum("hik,jkh->hij", x, right, preferred_element_type=jnp.float32)
        return scale(spread_of(contracted), 0)

    next_left, left = lax.optimization_barrier((next_left, left))
    left = with_layout_constraint(left.transpose(2, 0, 1), Layout(major_to_minor=(0, 1, 2)))
    next_left, scaled = gather_col(next_left, places, left, main_tile)
    next_left = next_left.reshape(2 * tile, tile, hidden)
    current = finish(pair_rep, scaled, gate, w_out[0])
    gate = gate_of(norm_in(current, 1), 1).reshape(current.shape)
    kept = lax.optimization_barrier(jnp.stack([gate, current.astype(jnp.float32)]))

    contracted = jnp.einsum(
        "kih,kjh->hij", next_left, next_right, preferred_element_type=jnp.float32
    )
    return finish(kept[1], scale(spread_of(contracted), 1), kept[0], w_out[1])


def solution(mesh):
    placed = (P("row", "col", None), P(), P(), P(), P(), P(), P(), P(), P(), P(), P())
    return jax.shard_map(
        body, mesh=mesh, in_specs=placed, out_specs=P("row", "col", None), check_vma=False
    )
```

```python
import jax
import jax.numpy as jnp
from jax import lax
from jax.experimental.layout import Layout, with_layout_constraint
from jax.sharding import PartitionSpec as P


def layer_norm(values, ln_gain, ln_bias):
    values = values.astype(jnp.float32)
    average = jnp.mean(values, axis=-1, keepdims=True)
    centred = values - average
    variance = jnp.mean(centred * centred, axis=-1, keepdims=True)
    return centred * lax.rsqrt(variance + 1e-05) * ln_gain + ln_bias


def gate_project(normed, keep, weight_proj, weight_gate):
    flat = normed.reshape(-1, normed.shape[-1])
    projected = jnp.dot(flat, weight_proj, preferred_element_type=jnp.float32)
    gate_logit = jnp.dot(flat, weight_gate, preferred_element_type=jnp.float32)
    gated = jax.nn.sigmoid(gate_logit) * projected * keep[:, None]
    return gated.astype(jnp.bfloat16).reshape(normed.shape[0], normed.shape[1], -1)


def out_gate(normed, w_outgate):
    flat = normed.reshape(-1, normed.shape[-1])
    return jax.nn.sigmoid(jnp.dot(flat, w_outgate, preferred_element_type=jnp.float32))


def spread_of(contracted):
    return contracted, jnp.mean(contracted, axis=0, keepdims=True)


def rescale(contracted, average, out_gain, out_bias):
    centred = contracted - average
    variance = jnp.mean(centred * centred, axis=0, keepdims=True)
    scaled = centred * lax.rsqrt(variance + 1e-05) * out_gain[:, None, None] + out_bias[:, None, None]
    return scaled.astype(jnp.bfloat16)


def finish(current, scaled, gate, w_out):
    branch = jnp.einsum("hij,hc->ijc", scaled, w_out, preferred_element_type=jnp.float32)
    updated = current.astype(jnp.float32) + branch * gate.reshape(branch.shape)
    return updated.astype(jnp.bfloat16)


def swap(x, axis, bits):
    n = lax.axis_size(axis)
    return lax.ppermute(x, axis, [(p, p ^ bits) for p in range(n)])


def put(buffer, x, *at):
    at = at + (jnp.uint32(0),) * x.ndim
    return lax.dynamic_update_slice(buffer, x.reshape((1,) * (len(at) - x.ndim) + x.shape), at)


def gather_col(piece, places, meanwhile=(), second=lambda x: x):
    half, other_half, ring, core, other_core = places
    pair = jnp.zeros((2,) + piece.shape, piece.dtype)
    pair = put(put(pair, piece, half), swap(piece, "col", 2), other_half)
    pair, meanwhile = lax.optimization_barrier((pair, meanwhile))
    four = put(jnp.zeros((4,) + pair.shape, piece.dtype), pair, ring[0])
    for d in (2, 1, 3):
        four = put(four, swap(pair, "col", 4 * d), ring[d])
    four, meanwhile = lax.optimization_barrier((four, second(meanwhile)))
    whole = jnp.zeros((2,) + four.shape, piece.dtype)
    whole = put(put(whole, four, core), swap(four, "col", 1), other_core)
    return jnp.moveaxis(whole, 0, 2).reshape((16,) + piece.shape), meanwhile


def transpose_devices(x):
    n = lax.axis_size("row")
    pairs = [(a * n + b, b * n + a) for a in range(n) for b in range(n)]
    return lax.ppermute(x, ("row", "col"), pairs)


def body(
    pair_rep,
    tok_mask,
    windows,
    in_gain,
    in_bias,
    w_proj,
    w_gate,
    out_gain,
    out_bias,
    w_out,
    w_outgate,
):
    tile = pair_rep.shape[0]
    width = pair_rep.shape[2]
    hidden = w_out.shape[1]
    n = lax.axis_size("row")
    part = tile // n
    row_idx = lax.axis_index("row")
    col_idx = lax.axis_index("col")

    def pick(stacked, update):
        return [
            lax.dynamic_index_in_dim(stacked, windows[update, slot], 0, keepdims=False)
            for slot in range(2)
        ]

    def norm_in(values, update):
        return layer_norm(values, in_gain[update], in_bias[update]).astype(jnp.bfloat16)

    def gate_of(normed, update):
        return out_gate(normed, w_outgate[update])

    def scale(made, update):
        return rescale(*made, out_gain[update], out_bias[update])

    row = row_idx.astype(jnp.uint32)
    col = col_idx.astype(jnp.uint32)
    zero = jnp.uint32(0)
    keeps = tok_mask.astype(jnp.float32).reshape(n, tile)

    def keep_of(block):
        return lax.dynamic_slice(keeps, (block.astype(jnp.uint32), zero), (1, tile))[0]

    def part_of(keep, place):
        return lax.dynamic_slice(keep, (place * part,), (part,))

    window_keep = jnp.concatenate([keep_of(windows[0, slot]) for slot in range(2)])
    rows_keep = jnp.concatenate([part_of(keep_of(windows[1, slot]), row) for slot in range(2)])
    band_keep = (part_of(keep_of(row), col)[:, None] * window_keep[None, :]).reshape(-1)
    moved_keep = (part_of(keep_of(col), row)[:, None] * window_keep[None, :]).reshape(-1)
    rows_keep = (rows_keep[:, None] * keep_of(col)[None, :]).reshape(-1)
    half, core = (col >> 1) & 1, col & 1
    places = (half, half ^ 1, [(col >> 2) ^ d for d in range(4)], core, core ^ 1)

    pieces = lax.all_to_all(pair_rep.reshape(n, part, tile, width), "col", 0, 0, tiled=True)
    pieces, places, band_keep, moved_keep, rows_keep = lax.optimization_barrier(
        (pieces, places, band_keep, moved_keep, rows_keep)
    )
    band = jnp.concatenate(pick(pieces, 0), axis=1)
    band = norm_in(band, 0)
    moved = transpose_devices(band)
    source, band = lax.optimization_barrier((pair_rep, band))
    gate = gate_of(norm_in(source, 0), 0)
    left_own = gate_project(band, band_keep, w_proj[0][:, :hidden], w_gate[0][:, :hidden])
    rows = pair_rep.reshape(n, part, tile, width)
    chunks = jnp.pad(rows, ((0, 0), (0, 0), (2 * tile, 0), (0, 0)))
    moved, gate, left_own, chunks = lax.optimization_barrier((moved, gate, left_own, chunks))
    gated = gate_project(moved, moved_keep, w_proj[0], w_gate[0])
    left_moved, right_moved = gated[..., :hidden], gated[..., hidden:]

    spread = jnp.broadcast_to(right_moved, (n,) + right_moved.shape)
    chunks = lax.dynamic_update_slice(chunks, spread, (0, 0, 0, 0))
    chunks, left_own = lax.optimization_barrier((chunks, left_own))
    chunks = lax.all_to_all(chunks, "row", 0, 0, tiled=True)
    rows = pick(chunks[:, :, 2 * tile :], 1)
    chunks, rows = lax.optimization_barrier((chunks, rows))
    rows = jnp.concatenate(rows, axis=0)
    right = chunks[:, :, : 2 * tile].reshape(tile, 2 * tile, hidden)
    lefts, _ = gather_col(jnp.stack([left_own, left_moved]), places)
    left = lefts[:, 0].reshape(tile, 2 * tile, hidden)
    left_rows = jnp.concatenate(pick(lefts[:, 1], 1), axis=0)

    contracted = jnp.einsum("ikh,jkh->hij", left_rows, right, preferred_element_type=jnp.float32)
    scaled = scale(spread_of(contracted), 0)
    rows = finish(rows, scaled, gate_of(norm_in(rows, 0), 0), w_out[0])
    gated = gate_project(norm_in(rows, 1), rows_keep, w_proj[1], w_gate[1])
    next_left = transpose_devices(gated[..., :hidden])
    copies = jnp.broadcast_to(gated[..., hidden:], (n, 2 * part, tile, hidden))
    next_right = lax.all_to_all(copies, "row", 0, 0, tiled=True).reshape(2 * tile, tile, hidden)

    def main_tile(x):
        contracted = jnp.einsum("hik,jkh->hij", x, right, preferred_element_type=jnp.float32)
        return scale(spread_of(contracted), 0)

    next_left, left = lax.optimization_barrier((next_left, left))
    left = with_layout_constraint(left.transpose(2, 0, 1), Layout(major_to_minor=(0, 1, 2)))
    next_left, scaled = gather_col(next_left, places, left, main_tile)
    next_left = next_left.reshape(2 * tile, tile, hidden)
    current = finish(pair_rep, scaled, gate, w_out[0])
    gate = gate_of(norm_in(current, 1), 1).reshape(current.shape)
    kept = lax.optimization_barrier(jnp.stack([gate, current.astype(jnp.float32)]))

    contracted = jnp.einsum(
        "kih,kjh->hij", next_left, next_right, preferred_element_type=jnp.float32
    )
    return finish(kept[1], scale(spread_of(contracted), 1), kept[0], w_out[1])


def solution(mesh):
    placed = (P("row", "col", None), P(), P(), P(), P(), P(), P(), P(), P(), P(), P())
    return jax.shard_map(
        body, mesh=mesh, in_specs=placed, out_specs=P("row", "col", None), check_vma=False
    )
```

```python
import jax
import jax.numpy as jnp
from jax import lax
from jax.experimental.layout import Layout, with_layout_constraint
from jax.sharding import PartitionSpec as P


def layer_norm(values, ln_gain, ln_bias):
    values = values.astype(jnp.float32)
    average = jnp.mean(values, axis=-1, keepdims=True)
    centred = values - average
    variance = jnp.mean(centred * centred, axis=-1, keepdims=True)
    return centred * lax.rsqrt(variance + 1e-05) * ln_gain + ln_bias


def gate_project(normed, keep, weight_proj, weight_gate):
    flat = normed.reshape(-1, normed.shape[-1])
    projected = jnp.dot(flat, weight_proj, preferred_element_type=jnp.float32)
    gate_logit = jnp.dot(flat, weight_gate, preferred_element_type=jnp.float32)
    gated = jax.nn.sigmoid(gate_logit) * projected * keep[:, None]
    return gated.astype(jnp.bfloat16).reshape(normed.shape[0], normed.shape[1], -1)


def out_gate(normed, w_outgate):
    flat = normed.reshape(-1, normed.shape[-1])
    return jax.nn.sigmoid(jnp.dot(flat, w_outgate, preferred_element_type=jnp.float32))


def spread_of(contracted):
    return contracted, jnp.mean(contracted, axis=0, keepdims=True)


def rescale(contracted, average, out_gain, out_bias):
    centred = contracted - average
    variance = jnp.mean(centred * centred, axis=0, keepdims=True)
    scaled = centred * lax.rsqrt(variance + 1e-05) * out_gain[:, None, None] + out_bias[:, None, None]
    return scaled.astype(jnp.bfloat16)


def finish(current, scaled, gate, w_out):
    branch = jnp.einsum("hij,hc->ijc", scaled, w_out, preferred_element_type=jnp.float32)
    updated = current.astype(jnp.float32) + branch * gate.reshape(branch.shape)
    return updated.astype(jnp.bfloat16)


def swap(x, axis, bits):
    n = lax.axis_size(axis)
    return lax.ppermute(x, axis, [(p, p ^ bits) for p in range(n)])


def put(buffer, x, *at):
    at = at + (jnp.uint32(0),) * x.ndim
    return lax.dynamic_update_slice(buffer, x.reshape((1,) * (len(at) - x.ndim) + x.shape), at)


def gather_col(piece, places, meanwhile=(), second=lambda x: x):
    half, other_half, ring, core, other_core = places
    pair = jnp.zeros((2,) + piece.shape, piece.dtype)
    pair = put(put(pair, piece, half), swap(piece, "col", 2), other_half)
    pair, meanwhile = lax.optimization_barrier((pair, meanwhile))
    four = put(jnp.zeros((4,) + pair.shape, piece.dtype), pair, ring[0])
    for d in (2, 1, 3):
        four = put(four, swap(pair, "col", 4 * d), ring[d])
    four, meanwhile = lax.optimization_barrier((four, second(meanwhile)))
    whole = jnp.zeros((2,) + four.shape, piece.dtype)
    whole = put(put(whole, four, core), swap(four, "col", 1), other_core)
    return jnp.moveaxis(whole, 0, 2).reshape((16,) + piece.shape), meanwhile


def transpose_devices(x):
    n = lax.axis_size("row")
    pairs = [(a * n + b, b * n + a) for a in range(n) for b in range(n)]
    return lax.ppermute(x, ("row", "col"), pairs)


def body(
    pair_rep,
    tok_mask,
    windows,
    in_gain,
    in_bias,
    w_proj,
    w_gate,
    out_gain,
    out_bias,
    w_out,
    w_outgate,
):
    tile = pair_rep.shape[0]
    width = pair_rep.shape[2]
    hidden = w_out.shape[1]
    n = lax.axis_size("row")
    part = tile // n
    row_idx = lax.axis_index("row")
    col_idx = lax.axis_index("col")

    def pick(stacked, update):
        return [
            lax.dynamic_index_in_dim(stacked, windows[update, slot], 0, keepdims=False)
            for slot in range(2)
        ]

    def norm_in(values, update):
        return layer_norm(values, in_gain[update], in_bias[update]).astype(jnp.bfloat16)

    def gate_of(normed, update):
        return out_gate(normed, w_outgate[update])

    def scale(made, update):
        return rescale(*made, out_gain[update], out_bias[update])

    row = row_idx.astype(jnp.uint32)
    col = col_idx.astype(jnp.uint32)
    zero = jnp.uint32(0)
    keeps = tok_mask.astype(jnp.float32).reshape(n, tile)

    def keep_of(block):
        return lax.dynamic_slice(keeps, (block.astype(jnp.uint32), zero), (1, tile))[0]

    def part_of(keep, place):
        return lax.dynamic_slice(keep, (place * part,), (part,))

    window_keep = jnp.concatenate([keep_of(windows[0, slot]) for slot in range(2)])
    rows_keep = jnp.concatenate([part_of(keep_of(windows[1, slot]), row) for slot in range(2)])
    band_keep = (part_of(keep_of(row), col)[:, None] * window_keep[None, :]).reshape(-1)
    moved_keep = (part_of(keep_of(col), row)[:, None] * window_keep[None, :]).reshape(-1)
    rows_keep = (rows_keep[:, None] * keep_of(col)[None, :]).reshape(-1)
    half, core = (col >> 1) & 1, col & 1
    places = (half, half ^ 1, [(col >> 2) ^ d for d in range(4)], core, core ^ 1)

    pieces = lax.all_to_all(pair_rep.reshape(n, part, tile, width), "col", 0, 0, tiled=True)
    pieces, places, band_keep, moved_keep, rows_keep = lax.optimization_barrier(
        (pieces, places, band_keep, moved_keep, rows_keep)
    )
    band = jnp.concatenate(pick(pieces, 0), axis=1)
    band = norm_in(band, 0)
    moved = transpose_devices(band)
    source, band = lax.optimization_barrier((pair_rep, band))
    gate = gate_of(norm_in(source, 0), 0)
    left_own = gate_project(band, band_keep, w_proj[0][:, :hidden], w_gate[0][:, :hidden])
    moved, gate, left_own = lax.optimization_barrier((moved, gate, left_own))
    gated = gate_project(moved, moved_keep, w_proj[0], w_gate[0])
    left_moved, right_moved = gated[..., :hidden], gated[..., hidden:]

    rows = pair_rep.reshape(n, part, tile, width)
    chunks = jnp.concatenate([jnp.broadcast_to(right_moved, (n,) + right_moved.shape), rows], axis=2)
    chunks, left_own = lax.optimization_barrier((chunks, left_own))
    chunks = lax.all_to_all(chunks, "row", 0, 0, tiled=True)
    rows = pick(chunks[:, :, 2 * tile :], 1)
    chunks, rows = lax.optimization_barrier((chunks, rows))
    rows = jnp.concatenate(rows, axis=0)
    right = chunks[:, :, : 2 * tile].reshape(tile, 2 * tile, hidden)
    lefts, _ = gather_col(jnp.stack([left_own, left_moved]), places)
    left = lefts[:, 0].reshape(tile, 2 * tile, hidden).transpose(2, 0, 1)
    left = with_layout_constraint(left, Layout(major_to_minor=(0, 1, 2)))
    left_rows = jnp.concatenate(pick(lefts[:, 1], 1), axis=0)
    left, left_rows = lax.optimization_barrier((left, left_rows))

    contracted = jnp.einsum("ikh,jkh->hij", left_rows, right, preferred_element_type=jnp.float32)
    scaled = scale(spread_of(contracted), 0)
    rows = finish(rows, scaled, gate_of(norm_in(rows, 0), 0), w_out[0])
    gated = gate_project(norm_in(rows, 1), rows_keep, w_proj[1], w_gate[1])
    next_left = transpose_devices(gated[..., :hidden])
    copies = jnp.broadcast_to(gated[..., hidden:], (n, 2 * part, tile, hidden))
    next_right = lax.all_to_all(copies, "row", 0, 0, tiled=True).reshape(2 * tile, tile, hidden)

    def main_tile(x):
        contracted = jnp.einsum("hik,jkh->hij", x, right, preferred_element_type=jnp.float32)
        return scale(spread_of(contracted), 0)

    next_left, left = lax.optimization_barrier((next_left, left))
    next_left, scaled = gather_col(next_left, places, left, main_tile)
    next_left = next_left.reshape(2 * tile, tile, hidden)
    current = finish(pair_rep, scaled, gate, w_out[0])
    gate = gate_of(norm_in(current, 1), 1).reshape(current.shape)
    kept = lax.optimization_barrier(jnp.stack([gate, current.astype(jnp.float32)]))

    contracted = jnp.einsum(
        "kih,kjh->hij", next_left, next_right, preferred_element_type=jnp.float32
    )
    return finish(kept[1], scale(spread_of(contracted), 1), kept[0], w_out[1])


def solution(mesh):
    placed = (P("row", "col", None), P(), P(), P(), P(), P(), P(), P(), P(), P(), P())
    return jax.shard_map(
        body, mesh=mesh, in_specs=placed, out_specs=P("row", "col", None), check_vma=False
    )
```

```python
import jax
import jax.numpy as jnp
from jax import lax
from jax.experimental.layout import Layout, with_layout_constraint
from jax.sharding import PartitionSpec as P


def layer_norm(values, ln_gain, ln_bias):
    values = values.astype(jnp.float32)
    average = jnp.mean(values, axis=-1, keepdims=True)
    centred = values - average
    variance = jnp.mean(centred * centred, axis=-1, keepdims=True)
    return centred * lax.rsqrt(variance + 1e-05) * ln_gain + ln_bias


def gate_project(normed, keep, weight_proj, weight_gate):
    flat = normed.reshape(-1, normed.shape[-1])
    projected = jnp.dot(flat, weight_proj, preferred_element_type=jnp.float32)
    gate_logit = jnp.dot(flat, weight_gate, preferred_element_type=jnp.float32)
    gated = jax.nn.sigmoid(gate_logit) * projected * keep[:, None]
    return gated.astype(jnp.bfloat16).reshape(normed.shape[0], normed.shape[1], -1)


def out_gate(normed, w_outgate):
    flat = normed.reshape(-1, normed.shape[-1])
    return jax.nn.sigmoid(jnp.dot(flat, w_outgate, preferred_element_type=jnp.float32))


def spread_of(contracted):
    return contracted, jnp.mean(contracted, axis=0, keepdims=True)


def rescale(contracted, average, out_gain, out_bias):
    centred = contracted - average
    variance = jnp.mean(centred * centred, axis=0, keepdims=True)
    scaled = centred * lax.rsqrt(variance + 1e-05) * out_gain[:, None, None] + out_bias[:, None, None]
    return scaled.astype(jnp.bfloat16)


def finish(current, scaled, gate, w_out):
    branch = jnp.einsum("hij,hc->ijc", scaled, w_out, preferred_element_type=jnp.float32)
    updated = current.astype(jnp.float32) + branch * gate.reshape(branch.shape)
    return updated.astype(jnp.bfloat16)


def swap(x, axis, bits):
    n = lax.axis_size(axis)
    return lax.ppermute(x, axis, [(p, p ^ bits) for p in range(n)])


def put(buffer, x, *at):
    at = at + (jnp.uint32(0),) * x.ndim
    return lax.dynamic_update_slice(buffer, x.reshape((1,) * (len(at) - x.ndim) + x.shape), at)


def gather_col(piece, places, meanwhile=(), second=lambda x: x):
    half, other_half, ring, core, other_core = places
    pair = jnp.zeros((2,) + piece.shape, piece.dtype)
    pair = put(put(pair, piece, half), swap(piece, "col", 2), other_half)
    pair, meanwhile = lax.optimization_barrier((pair, meanwhile))
    four = put(jnp.zeros((4,) + pair.shape, piece.dtype), pair, ring[0])
    for d in (2, 1, 3):
        four = put(four, swap(pair, "col", 4 * d), ring[d])
    four, meanwhile = lax.optimization_barrier((four, second(meanwhile)))
    whole = jnp.zeros((2,) + four.shape, piece.dtype)
    whole = put(put(whole, four, core), swap(four, "col", 1), other_core)
    return jnp.moveaxis(whole, 0, 2).reshape((16,) + piece.shape), meanwhile


def transpose_devices(x):
    n = lax.axis_size("row")
    pairs = [(a * n + b, b * n + a) for a in range(n) for b in range(n)]
    return lax.ppermute(x, ("row", "col"), pairs)


def body(
    pair_rep,
    tok_mask,
    windows,
    in_gain,
    in_bias,
    w_proj,
    w_gate,
    out_gain,
    out_bias,
    w_out,
    w_outgate,
):
    tile = pair_rep.shape[0]
    width = pair_rep.shape[2]
    hidden = w_out.shape[1]
    n = lax.axis_size("row")
    part = tile // n
    row_idx = lax.axis_index("row")
    col_idx = lax.axis_index("col")

    def pick(stacked, update):
        return [
            lax.dynamic_index_in_dim(stacked, windows[update, slot], 0, keepdims=False)
            for slot in range(2)
        ]

    def norm_in(values, update):
        return layer_norm(values, in_gain[update], in_bias[update]).astype(jnp.bfloat16)

    def gate_of(normed, update):
        return out_gate(normed, w_outgate[update])

    def scale(made, update):
        return rescale(*made, out_gain[update], out_bias[update])

    row = row_idx.astype(jnp.uint32)
    col = col_idx.astype(jnp.uint32)
    zero = jnp.uint32(0)
    keeps = tok_mask.astype(jnp.float32).reshape(n, tile)

    def keep_of(block):
        return lax.dynamic_slice(keeps, (block.astype(jnp.uint32), zero), (1, tile))[0]

    def part_of(keep, place):
        return lax.dynamic_slice(keep, (place * part,), (part,))

    window_keep = jnp.concatenate([keep_of(windows[0, slot]) for slot in range(2)])
    rows_keep = jnp.concatenate([part_of(keep_of(windows[1, slot]), row) for slot in range(2)])
    band_keep = (part_of(keep_of(row), col)[:, None] * window_keep[None, :]).reshape(-1)
    moved_keep = (part_of(keep_of(col), row)[:, None] * window_keep[None, :]).reshape(-1)
    rows_keep = (rows_keep[:, None] * keep_of(col)[None, :]).reshape(-1)
    half, core = (col >> 1) & 1, col & 1
    places = (half, half ^ 1, [(col >> 2) ^ d for d in range(4)], core, core ^ 1)

    pieces = lax.all_to_all(pair_rep.reshape(n, part, tile, width), "col", 0, 0, tiled=True)
    pieces, places, band_keep, moved_keep, rows_keep = lax.optimization_barrier(
        (pieces, places, band_keep, moved_keep, rows_keep)
    )
    band = jnp.concatenate(pick(pieces, 0), axis=1)
    band = norm_in(band, 0)
    moved = transpose_devices(band)
    source, band = lax.optimization_barrier((pair_rep, band))
    gate = gate_of(norm_in(source, 0), 0)
    left_own = gate_project(band, band_keep, w_proj[0][:, :hidden], w_gate[0][:, :hidden])
    moved, gate, left_own = lax.optimization_barrier((moved, gate, left_own))
    gated = gate_project(moved, moved_keep, w_proj[0], w_gate[0])
    left_moved, right_moved = gated[..., :hidden], gated[..., hidden:]

    rows = pair_rep.reshape(n, part, tile, width)
    chunks = jnp.concatenate([jnp.broadcast_to(right_moved, (n,) + right_moved.shape), rows], axis=2)
    chunks, left_own = lax.optimization_barrier((chunks, left_own))
    chunks = lax.all_to_all(chunks, "row", 0, 0, tiled=True)
    rows = pick(chunks[:, :, 2 * tile :], 1)
    chunks, rows = lax.optimization_barrier((chunks, rows))
    rows = jnp.concatenate(rows, axis=0)
    right = chunks[:, :, : 2 * tile].reshape(tile, 2 * tile, hidden)
    lefts, _ = gather_col(jnp.stack([left_own, left_moved]), places)
    left = lefts[:, 0].reshape(tile, 2 * tile, hidden)
    left_rows = jnp.concatenate(pick(lefts[:, 1], 1), axis=0)

    contracted = jnp.einsum("ikh,jkh->hij", left_rows, right, preferred_element_type=jnp.float32)
    scaled = scale(spread_of(contracted), 0)
    rows = finish(rows, scaled, gate_of(norm_in(rows, 0), 0), w_out[0])
    gated = gate_project(norm_in(rows, 1), rows_keep, w_proj[1], w_gate[1])
    next_left = transpose_devices(gated[..., :hidden])
    copies = jnp.broadcast_to(gated[..., hidden:], (n, 2 * part, tile, hidden))
    next_right = lax.all_to_all(copies, "row", 0, 0, tiled=True).reshape(2 * tile, tile, hidden)

    def main_tile(x):
        contracted = jnp.einsum("hik,jkh->hij", x, right, preferred_element_type=jnp.float32)
        return scale(spread_of(contracted), 0)

    next_left, left = lax.optimization_barrier((next_left, left))
    left = with_layout_constraint(left.transpose(2, 0, 1), Layout(major_to_minor=(0, 1, 2)))
    next_left, scaled = gather_col(next_left, places, left, main_tile)
    next_left = next_left.reshape(2 * tile, tile, hidden)
    current = finish(pair_rep, scaled, gate, w_out[0])
    gate = gate_of(norm_in(current, 1), 1)

    contracted = jnp.einsum(
        "kih,kjh->hij", next_left, next_right, preferred_element_type=jnp.float32
    )
    return finish(current, scale(spread_of(contracted), 1), gate, w_out[1])


def solution(mesh):
    placed = (P("row", "col", None), P(), P(), P(), P(), P(), P(), P(), P(), P(), P())
    return jax.shard_map(
        body, mesh=mesh, in_specs=placed, out_specs=P("row", "col", None), check_vma=False
    )
```

```python
import jax
import jax.numpy as jnp
from jax import lax
from jax.experimental.layout import Layout, with_layout_constraint
from jax.sharding import PartitionSpec as P


def layer_norm(values, ln_gain, ln_bias):
    values = values.astype(jnp.float32)
    average = jnp.mean(values, axis=-1, keepdims=True)
    centred = values - average
    variance = jnp.mean(centred * centred, axis=-1, keepdims=True)
    return centred * lax.rsqrt(variance + 1e-05) * ln_gain + ln_bias


def gate_project(normed, keep, weight_proj, weight_gate):
    flat = normed.reshape(-1, normed.shape[-1])
    projected = jnp.dot(flat, weight_proj, preferred_element_type=jnp.float32)
    gate_logit = jnp.dot(flat, weight_gate, preferred_element_type=jnp.float32)
    gated = jax.nn.sigmoid(gate_logit) * projected * keep[:, None]
    return gated.astype(jnp.bfloat16).reshape(normed.shape[0], normed.shape[1], -1)


def out_gate(normed, w_outgate):
    flat = normed.reshape(-1, normed.shape[-1])
    return jax.nn.sigmoid(jnp.dot(flat, w_outgate, preferred_element_type=jnp.float32))


def spread_of(contracted):
    return contracted, jnp.mean(contracted, axis=0, keepdims=True)


def rescale(contracted, average, out_gain, out_bias):
    centred = contracted - average
    variance = jnp.mean(centred * centred, axis=0, keepdims=True)
    scaled = centred * lax.rsqrt(variance + 1e-05) * out_gain[:, None, None] + out_bias[:, None, None]
    return scaled.astype(jnp.bfloat16)


def finish(current, scaled, gate, w_out):
    branch = jnp.einsum("hij,hc->ijc", scaled, w_out, preferred_element_type=jnp.float32)
    updated = current.astype(jnp.float32) + branch * gate.reshape(branch.shape)
    return updated.astype(jnp.bfloat16)


def swap(x, axis, bits):
    n = lax.axis_size(axis)
    return lax.ppermute(x, axis, [(p, p ^ bits) for p in range(n)])


def put(buffer, x, *at):
    at = at + (jnp.uint32(0),) * x.ndim
    return lax.dynamic_update_slice(buffer, x.reshape((1,) * (len(at) - x.ndim) + x.shape), at)


def gather_col(piece, places, meanwhile=(), second=lambda x: x):
    half, other_half, ring, core, other_core = places
    pair = jnp.zeros((2,) + piece.shape, piece.dtype)
    pair = put(put(pair, piece, half), swap(piece, "col", 2), other_half)
    pair, meanwhile = lax.optimization_barrier((pair, meanwhile))
    four = put(jnp.zeros((4,) + pair.shape, piece.dtype), pair, ring[0])
    for d in (2, 1, 3):
        four = put(four, swap(pair, "col", 4 * d), ring[d])
    four, meanwhile = lax.optimization_barrier((four, second(meanwhile)))
    whole = jnp.zeros((2,) + four.shape, piece.dtype)
    whole = put(put(whole, four, core), swap(four, "col", 1), other_core)
    return jnp.moveaxis(whole, 0, 2).reshape((16,) + piece.shape), meanwhile


def transpose_devices(x):
    n = lax.axis_size("row")
    pairs = [(a * n + b, b * n + a) for a in range(n) for b in range(n)]
    return lax.ppermute(x, ("row", "col"), pairs)


def body(
    pair_rep,
    tok_mask,
    windows,
    in_gain,
    in_bias,
    w_proj,
    w_gate,
    out_gain,
    out_bias,
    w_out,
    w_outgate,
):
    tile = pair_rep.shape[0]
    width = pair_rep.shape[2]
    hidden = w_out.shape[1]
    n = lax.axis_size("row")
    part = tile // n
    row_idx = lax.axis_index("row")
    col_idx = lax.axis_index("col")

    def pick(stacked, update):
        return [
            lax.dynamic_index_in_dim(stacked, windows[update, slot], 0, keepdims=False)
            for slot in range(2)
        ]

    def norm_in(values, update):
        return layer_norm(values, in_gain[update], in_bias[update]).astype(jnp.bfloat16)

    def gate_of(normed, update):
        return out_gate(normed, w_outgate[update])

    def scale(made, update):
        return rescale(*made, out_gain[update], out_bias[update])

    row = row_idx.astype(jnp.uint32)
    col = col_idx.astype(jnp.uint32)
    zero = jnp.uint32(0)
    keeps = tok_mask.astype(jnp.float32).reshape(n, tile)

    def keep_of(block):
        return lax.dynamic_slice(keeps, (block.astype(jnp.uint32), zero), (1, tile))[0]

    def part_of(keep, place):
        return lax.dynamic_slice(keep, (place * part,), (part,))

    window_keep = jnp.concatenate([keep_of(windows[0, slot]) for slot in range(2)])
    rows_keep = jnp.concatenate([part_of(keep_of(windows[1, slot]), row) for slot in range(2)])
    band_keep = (part_of(keep_of(row), col)[:, None] * window_keep[None, :]).reshape(-1)
    moved_keep = (part_of(keep_of(col), row)[:, None] * window_keep[None, :]).reshape(-1)
    rows_keep = (rows_keep[:, None] * keep_of(col)[None, :]).reshape(-1)
    half, core = (col >> 1) & 1, col & 1
    places = (half, half ^ 1, [(col >> 2) ^ d for d in range(4)], core, core ^ 1)

    pieces = lax.all_to_all(pair_rep.reshape(n, part, tile, width), "col", 0, 0, tiled=True)
    pieces, places, band_keep, moved_keep, rows_keep = lax.optimization_barrier(
        (pieces, places, band_keep, moved_keep, rows_keep)
    )
    band = jnp.concatenate(pick(pieces, 0), axis=1)
    band = norm_in(band, 0)
    moved = transpose_devices(band)
    source, band = lax.optimization_barrier((pair_rep, band))
    gate = gate_of(norm_in(source, 0), 0)
    left_own = gate_project(band, band_keep, w_proj[0][:, :hidden], w_gate[0][:, :hidden])
    tiles, left_own = lax.optimization_barrier((pair_rep, left_own))
    shares = lax.all_to_all(tiles.reshape(n, part, tile, width), "row", 0, 0, tiled=True)
    moved, gate, left_own, shares = lax.optimization_barrier((moved, gate, left_own, shares))
    gated = gate_project(moved, moved_keep, w_proj[0], w_gate[0])
    left_moved, right_moved = gated[..., :hidden], gated[..., hidden:]

    chunks = jnp.broadcast_to(right_moved, (n,) + right_moved.shape)
    chunks, left_own = lax.optimization_barrier((chunks, left_own))
    chunks = lax.all_to_all(chunks, "row", 0, 0, tiled=True)
    rows = jnp.concatenate(pick(shares, 1), axis=0)
    right = chunks.reshape(tile, 2 * tile, hidden)
    lefts, _ = gather_col(jnp.stack([left_own, left_moved]), places)
    left = lefts[:, 0].reshape(tile, 2 * tile, hidden)
    left_rows = jnp.concatenate(pick(lefts[:, 1], 1), axis=0)

    contracted = jnp.einsum("ikh,jkh->hij", left_rows, right, preferred_element_type=jnp.float32)
    scaled = scale(spread_of(contracted), 0)
    rows = finish(rows, scaled, gate_of(norm_in(rows, 0), 0), w_out[0])
    gated = gate_project(norm_in(rows, 1), rows_keep, w_proj[1], w_gate[1])
    next_left = transpose_devices(gated[..., :hidden])
    copies = jnp.broadcast_to(gated[..., hidden:], (n, 2 * part, tile, hidden))
    next_right = lax.all_to_all(copies, "row", 0, 0, tiled=True).reshape(2 * tile, tile, hidden)

    def main_tile(x):
        contracted = jnp.einsum("hik,jkh->hij", x, right, preferred_element_type=jnp.float32)
        return scale(spread_of(contracted), 0)

    next_left, left = lax.optimization_barrier((next_left, left))
    left = with_layout_constraint(left.transpose(2, 0, 1), Layout(major_to_minor=(0, 1, 2)))
    next_left, scaled = gather_col(next_left, places, left, main_tile)
    next_left = next_left.reshape(2 * tile, tile, hidden)
    current = finish(pair_rep, scaled, gate, w_out[0])
    gate = gate_of(norm_in(current, 1), 1).reshape(current.shape)
    kept = lax.optimization_barrier(jnp.stack([gate, current.astype(jnp.float32)]))

    contracted = jnp.einsum(
        "kih,kjh->hij", next_left, next_right, preferred_element_type=jnp.float32
    )
    return finish(kept[1], scale(spread_of(contracted), 1), kept[0], w_out[1])


def solution(mesh):
    placed = (P("row", "col", None), P(), P(), P(), P(), P(), P(), P(), P(), P(), P())
    return jax.shard_map(
        body, mesh=mesh, in_specs=placed, out_specs=P("row", "col", None), check_vma=False
    )
```

```python
import jax
import jax.numpy as jnp
from jax import lax
from jax.experimental.layout import Layout, with_layout_constraint
from jax.sharding import PartitionSpec as P


def layer_norm(values, ln_gain, ln_bias):
    values = values.astype(jnp.float32)
    average = jnp.mean(values, axis=-1, keepdims=True)
    centred = values - average
    variance = jnp.mean(centred * centred, axis=-1, keepdims=True)
    return centred * lax.rsqrt(variance + 1e-05) * ln_gain + ln_bias


def gate_project(normed, keep, weight_proj, weight_gate):
    flat = normed.reshape(-1, normed.shape[-1])
    projected = jnp.dot(flat, weight_proj, preferred_element_type=jnp.float32)
    gate_logit = jnp.dot(flat, weight_gate, preferred_element_type=jnp.float32)
    gated = jax.nn.sigmoid(gate_logit) * projected * keep[:, None]
    return gated.astype(jnp.bfloat16).reshape(normed.shape[0], normed.shape[1], -1)


def out_gate(normed, w_outgate):
    flat = normed.reshape(-1, normed.shape[-1])
    return jax.nn.sigmoid(jnp.dot(flat, w_outgate, preferred_element_type=jnp.float32))


def spread_of(contracted):
    return contracted, jnp.mean(contracted, axis=0, keepdims=True)


def rescale(contracted, average, out_gain, out_bias):
    centred = contracted - average
    variance = jnp.mean(centred * centred, axis=0, keepdims=True)
    scaled = centred * lax.rsqrt(variance + 1e-05) * out_gain[:, None, None] + out_bias[:, None, None]
    return scaled.astype(jnp.bfloat16)


def finish(current, scaled, gate, w_out):
    branch = jnp.einsum("hij,hc->ijc", scaled, w_out, preferred_element_type=jnp.float32)
    updated = current.astype(jnp.float32) + branch * gate.reshape(branch.shape)
    return updated.astype(jnp.bfloat16)


def swap(x, axis, bits):
    n = lax.axis_size(axis)
    return lax.ppermute(x, axis, [(p, p ^ bits) for p in range(n)])


def put(buffer, x, *at):
    at = at + (jnp.uint32(0),) * x.ndim
    return lax.dynamic_update_slice(buffer, x.reshape((1,) * (len(at) - x.ndim) + x.shape), at)


def gather_col(piece, places, meanwhile=(), second=lambda x: x):
    half, other_half, ring, core, other_core = places
    pair = jnp.zeros((2,) + piece.shape, piece.dtype)
    pair = put(put(pair, piece, half), swap(piece, "col", 2), other_half)
    pair, meanwhile = lax.optimization_barrier((pair, meanwhile))
    four = put(jnp.zeros((4,) + pair.shape, piece.dtype), pair, ring[0])
    for d in (2, 1, 3):
        four = put(four, swap(pair, "col", 4 * d), ring[d])
    four, meanwhile = lax.optimization_barrier((four, second(meanwhile)))
    whole = jnp.zeros((2,) + four.shape, piece.dtype)
    whole = put(put(whole, four, core), swap(four, "col", 1), other_core)
    return jnp.moveaxis(whole, 0, 2).reshape((16,) + piece.shape), meanwhile


def transpose_devices(x):
    n = lax.axis_size("row")
    pairs = [(a * n + b, b * n + a) for a in range(n) for b in range(n)]
    return lax.ppermute(x, ("row", "col"), pairs)


def body(
    pair_rep,
    tok_mask,
    windows,
    in_gain,
    in_bias,
    w_proj,
    w_gate,
    out_gain,
    out_bias,
    w_out,
    w_outgate,
):
    tile = pair_rep.shape[0]
    width = pair_rep.shape[2]
    hidden = w_out.shape[1]
    n = lax.axis_size("row")
    part = tile // n
    row_idx = lax.axis_index("row")
    col_idx = lax.axis_index("col")

    def pick(stacked, update):
        return [
            lax.dynamic_index_in_dim(
                stacked, windows[update, slot], 0, keepdims=False, allow_negative_indices=update == 0
            )
            for slot in range(2)
        ]

    def norm_in(values, update):
        return layer_norm(values, in_gain[update], in_bias[update]).astype(jnp.bfloat16)

    def gate_of(normed, update):
        return out_gate(normed, w_outgate[update])

    def scale(made, update):
        return rescale(*made, out_gain[update], out_bias[update])

    row = row_idx.astype(jnp.uint32)
    col = col_idx.astype(jnp.uint32)
    zero = jnp.uint32(0)
    keeps = tok_mask.astype(jnp.float32).reshape(n, tile)

    def keep_of(block):
        return lax.dynamic_slice(keeps, (block.astype(jnp.uint32), zero), (1, tile))[0]

    def part_of(keep, place):
        return lax.dynamic_slice(keep, (place * part,), (part,))

    window_keep = jnp.concatenate([keep_of(windows[0, slot]) for slot in range(2)])
    rows_keep = jnp.concatenate([part_of(keep_of(windows[1, slot]), row) for slot in range(2)])
    band_keep = (part_of(keep_of(row), col)[:, None] * window_keep[None, :]).reshape(-1)
    moved_keep = (part_of(keep_of(col), row)[:, None] * window_keep[None, :]).reshape(-1)
    rows_keep = (rows_keep[:, None] * keep_of(col)[None, :]).reshape(-1)
    half, core = (col >> 1) & 1, col & 1
    places = (half, half ^ 1, [(col >> 2) ^ d for d in range(4)], core, core ^ 1)

    pieces = lax.all_to_all(pair_rep.reshape(n, part, tile, width), "col", 0, 0, tiled=True)
    pieces, places, band_keep, moved_keep, rows_keep = lax.optimization_barrier(
        (pieces, places, band_keep, moved_keep, rows_keep)
    )
    band = jnp.concatenate(pick(pieces, 0), axis=1)
    band = norm_in(band, 0)
    moved = transpose_devices(band)
    source, band = lax.optimization_barrier((pair_rep, band))
    gate = gate_of(norm_in(source, 0), 0)
    left_own = gate_project(band, band_keep, w_proj[0][:, :hidden], w_gate[0][:, :hidden])
    tiles, left_own = lax.optimization_barrier((pair_rep, left_own))
    shares = lax.all_to_all(tiles.reshape(n, part, tile, width), "row", 0, 0, tiled=True)
    moved, gate, left_own, shares = lax.optimization_barrier((moved, gate, left_own, shares))
    gated = gate_project(moved, moved_keep, w_proj[0], w_gate[0])
    left_moved, right_moved = gated[..., :hidden], gated[..., hidden:]

    chunks = jnp.broadcast_to(right_moved, (n,) + right_moved.shape)
    chunks, left_own = lax.optimization_barrier((chunks, left_own))
    chunks = lax.all_to_all(chunks, "row", 0, 0, tiled=True)
    rows = jnp.concatenate(pick(shares, 1), axis=0)
    right = chunks.reshape(tile, 2 * tile, hidden)
    lefts, _ = gather_col(jnp.stack([left_own, left_moved]), places)
    left = lefts[:, 0].reshape(tile, 2 * tile, hidden)
    left_rows = jnp.concatenate(pick(lefts[:, 1], 1), axis=0)

    contracted = jnp.einsum("ikh,jkh->hij", left_rows, right, preferred_element_type=jnp.float32)
    scaled = scale(spread_of(contracted), 0)
    rows = finish(rows, scaled, gate_of(norm_in(rows, 0), 0), w_out[0])
    gated = gate_project(norm_in(rows, 1), rows_keep, w_proj[1], w_gate[1])
    next_left = transpose_devices(gated[..., :hidden])
    copies = jnp.broadcast_to(gated[..., hidden:], (n, 2 * part, tile, hidden))
    next_right = lax.all_to_all(copies, "row", 0, 0, tiled=True).reshape(2 * tile, tile, hidden)

    def main_tile(x):
        contracted = jnp.einsum("hik,jkh->hij", x, right, preferred_element_type=jnp.float32)
        return scale(spread_of(contracted), 0)

    next_left, left = lax.optimization_barrier((next_left, left))
    left = with_layout_constraint(left.transpose(2, 0, 1), Layout(major_to_minor=(0, 1, 2)))
    next_left, scaled = gather_col(next_left, places, left, main_tile)
    next_left = next_left.reshape(2 * tile, tile, hidden)
    current = finish(pair_rep, scaled, gate, w_out[0])
    gate = gate_of(norm_in(current, 1), 1).reshape(current.shape)
    kept = lax.optimization_barrier(jnp.stack([gate, current.astype(jnp.float32)]))

    contracted = jnp.einsum(
        "kih,kjh->hij", next_left, next_right, preferred_element_type=jnp.float32
    )
    return finish(kept[1], scale(spread_of(contracted), 1), kept[0], w_out[1])


def solution(mesh):
    placed = (P("row", "col", None), P(), P(), P(), P(), P(), P(), P(), P(), P(), P())
    return jax.shard_map(
        body, mesh=mesh, in_specs=placed, out_specs=P("row", "col", None), check_vma=False
    )
```
